32 devices in a mesh: tm: 4 (over y, x), slab: 8 (over z, core).
Axes of the slice: x: 2, y: 2, z: 4, core: 2. Of those that a mesh axis runs over, the one named last changes fastest.
Arguments:
- eigvecs: float32 [4, 3, 3456, 2, 128], P('tm', None, 'slab'), may hold values from -6 to 6
- perambulator: float32 [512, 8, 2, 512], P('slab', 'tm'), may hold values from -0.015625 to 0.015625
- time_pairs: int32 [8, 2], P('tm'), may hold values from 0 to 3
- momenta: int32 [4, 3], replicated, may hold values from -2 to 2, as said below
Outputs:
- dressed: float32 [512, 8, 4, 2, 512], P('slab', 'tm')
The draws below stay inside these ranges and needn't reach their ends.
Inputs may be any that keep to these rules, and one draw needn't show every extreme that they name: `momenta`: every component of each momentum is nonzero.
All inputs are finite; a program needn't handle non-finite values.
Results may differ from the reference program's by a relative error of at most 0.0001.
Values sent between devices are 32-bit elements; how exact they have to be, the bound alone decides.
A program may use at most 64 MiB of HBM per device.

```python
import math
import jax
import jax.numpy as jnp
from jax import lax

NVEC = 128
NCOL = 3
LS = 48
NMOM = 4
NS = 512
NT = 4
NSITE = 3456
NPAIR = 8


def draw_momenta(key, part):
    magnitude = jax.random.randint(jax.random.fold_in(key, 11), (NMOM, 3), 1, 3)
    flips = jax.random.randint(jax.random.fold_in(key, 12), (NMOM, 3), 0, 2) * 2 - 1
    return (magnitude * flips).astype(jnp.int32)


def with_ends(result, key, least, high):
    extent = result.shape
    place = [jax.random.randint(jax.random.fold_in(key, axis), (), 0, extent[axis]) for axis in range(len(extent))]
    result = result.at[tuple(place)].set(least)
    longest = extent.index(max(extent))
    place[longest] = (place[longest] + 1) % extent[longest]
    return result.at[tuple(place)].set(high)


def shard_levels(key, dims, cuts, least, top_value):
    level = 1.0
    for position, parts in cuts:
        draws = jax.random.uniform(jax.random.fold_in(jax.random.fold_in(key, 6), position), (parts,), jnp.float32, least / len(cuts), top_value / len(cuts))
        level = level * jnp.repeat(jnp.exp(draws), dims[position] // parts).reshape((-1,) + (1,) * (len(dims) - 1 - position))
    return level


def noise(rng, shape, scale, limit, split=(), held_as=jnp.bfloat16):
    result = jax.random.normal(rng, shape, jnp.float32) * scale
    if len(split) > 0:
        result = shard_levels(rng, shape, split, -0.22, 0.18) * result
    return jnp.clip(result, min=-limit, max=limit).astype(held_as)


def setup_inputs(seed: int = 0) -> dict:
    key_of = jax.random.split(jax.random.key(seed), 5)
    eigvecs = noise(key_of[0], (NT, NCOL, NSITE, 2, NVEC), 1.0, 6.0, ((0, 4), (2, 8)), jnp.float32)
    perambulator = noise(key_of[1], (NS, NPAIR, 2, NS), (NS * NS // 2) ** -0.5, 0.015625, ((0, 8), (1, 4)), jnp.float32)
    time_pairs = with_ends(jax.random.randint(key_of[2], (NPAIR, 2), 0, NT), jax.random.fold_in(key_of[2], 1), 0, NT - 1).astype(jnp.int32)
    momenta = draw_momenta(jax.random.fold_in(key_of[4], 71), 0)
    return {"eigvecs": eigvecs, "perambulator": perambulator, "time_pairs": time_pairs, "momenta": momenta}


PRECISE = lax.Precision.HIGHEST
SPIN_MIX = ((1.0, 0.0, 1.0, 0.0), (0.0, 1.0, 0.0, 1.0), (1.0, 0.0, 1.0, 0.0), (0.0, 1.0, 0.0, 1.0))
CHIRAL = (1.0, 1.0, -1.0, -1.0)

def spin_tables():
    spin_mix = jnp.array(SPIN_MIX, jnp.float32)
    chiral = jnp.array(CHIRAL, jnp.float32)
    spin_dressed = chiral[:, None] * spin_mix * chiral[None, :]
    return (spin_mix, spin_dressed)

def phase_tables(momenta, site_ids):
    coords = jnp.stack([site_ids % LS, site_ids // LS % LS, site_ids // (LS * LS)])
    phase_turns = jnp.mod(lax.optimization_barrier(jnp.sum(momenta[:, :, None] * coords[None, :, :], axis=1)), LS)
    phase_angle = phase_turns.astype(jnp.float32) * (2.0 * math.pi / LS)
    return (jnp.cos(phase_angle), jnp.sin(phase_angle))

def elemental_terms(vectors, cosine_tab, sine_tab):
    local_times = vectors.shape[0]
    vec_count = vectors.shape[4]
    real_part = vectors[:, :, :, 0, :]
    imag_part = vectors[:, :, :, 1, :]
    left_rows = vectors.reshape(local_times, -1, vec_count)
    per_moment = []
    for mom_index in range(cosine_tab.shape[0]):
        cos_here = cosine_tab[mom_index][None, None, :, None]
        sin_here = sine_tab[mom_index][None, None, :, None]
        turned_re = cos_here * real_part - sin_here * imag_part
        turned_im = sin_here * real_part + cos_here * imag_part
        first_half = jnp.stack([turned_re, turned_im], axis=3).reshape(local_times, -1, vec_count)
        second_half = jnp.stack([turned_im, -turned_re], axis=3).reshape(local_times, -1, vec_count)
        right_cols = jnp.concatenate([first_half, second_half], axis=2)
        product = jnp.einsum('tki,tkj->tij', left_rows, right_cols, precision=PRECISE)
        per_moment.append(product.reshape(local_times, vec_count, 2, vec_count).transpose(0, 2, 1, 3))
    return jnp.stack(per_moment, axis=1)

def plain_dot(left_mat, right_mat):
    return jnp.dot(left_mat, right_mat, precision=PRECISE, preferred_element_type=jnp.float32)

def complex_dot(left_re, left_im, right_re, right_im):
    return (plain_dot(left_re, right_re) - plain_dot(left_im, right_im), plain_dot(left_re, right_im) + plain_dot(left_im, right_re))

def reference(eigvecs, perambulator, time_pairs, momenta):
    site_ids = jnp.arange(NSITE, dtype=jnp.int32)
    cosine_tab, sine_tab = phase_tables(momenta, site_ids)
    elementals = lax.map(lambda slice_vec: elemental_terms(slice_vec[None], cosine_tab, sine_tab)[0], eigvecs)
    elementals = elementals * (1.0 / math.sqrt(2.0 * NCOL * NSITE))
    spin_mix, spin_dressed = spin_tables()

    def dress_pair(index_pair):
        sink_elem = elementals[time_pairs[index_pair, 1]]
        source_elem = elementals[time_pairs[index_pair, 0]]
        peram_pair = lax.dynamic_index_in_dim(perambulator, index_pair, 1, keepdims=False)
        peram_re = peram_pair[:, 0, :].T
        peram_im = peram_pair[:, 1, :].T
        per_moment = []
        for mom_index in range(NMOM):
            outer_re = jnp.kron(spin_mix, sink_elem[mom_index, 0])
            outer_im = jnp.kron(spin_mix, sink_elem[mom_index, 1])
            dress_re = jnp.kron(spin_dressed, source_elem[mom_index, 0].T)
            dress_im = -jnp.kron(spin_dressed, source_elem[mom_index, 1].T)
            inner_re, inner_im = complex_dot(outer_re, outer_im, peram_re, peram_im)
            final_re, final_im = complex_dot(inner_re, inner_im, dress_re, dress_im)
            per_moment.append(jnp.stack([final_re.T, final_im.T], axis=1))
        return jnp.stack(per_moment, axis=1)
    stacked = lax.map(dress_pair, jnp.arange(NPAIR, dtype=jnp.int32))
    return jnp.transpose(stacked, (1, 0, 2, 3, 4))
```

```python
import functools
import math

import jax
import jax.numpy as jnp
from jax import lax
from jax.experimental import pallas as pl
from jax.experimental.pallas import tpu as pltpu
from jax.sharding import PartitionSpec as P

LS = 48
SLABS = 8
TIMES = 4
BF16 = jnp.bfloat16
F32 = jnp.float32
NN = (((1,), (0,)), ((), ()))
NT = (((1,), (1,)), ((), ()))


def split(value):
    high = value.astype(BF16)
    return high, (value - high.astype(F32)).astype(BF16)


def dot3(left, right, dims):
    def one(x, y):
        return lax.dot_general(x, y, dims, preferred_element_type=F32)

    return one(left[0], right[0]) + (one(left[0], right[1]) + one(left[1], right[0]))


def floor_div(value, by):
    return jnp.floor((value + 0.5) * (1.0 / by))


def gather_kernel(
    scale, mom_ref, eig_ref, per_ref, e_ref, d_ref,
    lh, ll, rh, rl, phase, part, r1, r2, h2, r3, psend, precv,
    send_sem, recv_sem, psend_sem, precv_sem,
):
    slab = lax.axis_index("slab")
    time = lax.axis_index("tm")
    core = slab % 2
    sub = (slab // 2) % 2
    sibling = slab + 1 - 2 * core
    near = slab + 2 - 4 * sub
    far = (slab + 4) % SLABS
    tm_peers = (time + 1 - 2 * (time % 2), (time + 2) % TIMES, TIMES - 1 - time)
    slab_peers = (sibling, near, far)

    barrier = pltpu.get_barrier_semaphore()
    for peer in slab_peers:
        pl.semaphore_signal(barrier, inc=1, device_id={"slab": peer}, device_id_type=pl.DeviceIdType.MESH)
    for peer in tm_peers:
        pl.semaphore_signal(barrier, inc=1, device_id={"tm": peer}, device_id_type=pl.DeviceIdType.MESH)

    pairs = psend.shape[0]
    cols = psend.shape[2]
    for k in range(pairs):
        for p in range(2):
            spins = [
                per_ref[pl.ds(k * 8 + t * 2 + p, cols, stride=8 * pairs), :] for t in range(4)
            ]
            psend[k, p, :, 0:128] = spins[0] + spins[2]
            psend[k, p, :, 128:256] = spins[1] + spins[3]

    pl.semaphore_wait(barrier, len(slab_peers) + len(tm_peers))

    def remote(src, dst, ssem, rsem, axis, peer):
        return pltpu.make_async_remote_copy(
            src_ref=src, dst_ref=dst, send_sem=ssem, recv_sem=rsem,
            device_id={axis: peer}, device_id_type=pl.DeviceIdType.MESH,
        )

    p_far = remote(psend, precv, psend_sem.at[0], precv_sem.at[0], "slab", far)
    p_far.start()
    p_core = remote(d_ref.at[core], d_ref.at[core], psend_sem.at[1], precv_sem.at[1], "slab", sibling)

    moms = mom_ref.shape[0]
    sites = phase.shape[0]
    site = (lax.broadcasted_iota(jnp.int32, (sites, 128), 0) + slab * sites).astype(F32)
    lane = lax.broadcasted_iota(jnp.int32, (sites, 128), 1)
    row = floor_div(site, LS)
    plane = floor_div(row, LS)
    coords = (site - LS * row, row - LS * plane, plane)
    turns = jnp.zeros((sites, 128), F32)
    for m in range(moms):
        mine = mom_ref[m, 0].astype(F32) * coords[0]
        mine = mine + mom_ref[m, 1].astype(F32) * coords[1]
        mine = mine + mom_ref[m, 2].astype(F32) * coords[2]
        turns = jnp.where(lane % moms == m, mine, turns)
    turns = turns - LS * floor_div(turns, LS)
    turns = jnp.where(lane >= moms, turns - LS / 4, turns)
    phase[...] = jnp.cos(turns * (2.0 * math.pi / LS))

    colours = eig_ref.shape[0] // (2 * sites)
    for c in range(colours):
        real = eig_ref[pl.ds(2 * sites * c, sites, stride=2), :]
        imag = eig_ref[pl.ds(2 * sites * c + 1, sites, stride=2), :]
        high, low = split(jnp.concatenate([real, imag], axis=1))
        lh[c * sites:(c + 1) * sites, :] = high
        ll[c * sites:(c + 1) * sites, :] = low

    def compute(m):
        cosine = phase[:, m:m + 1]
        sine = phase[:, moms + m:moms + m + 1]
        for c in range(colours):
            real = eig_ref[pl.ds(2 * sites * c, sites, stride=2), :]
            imag = eig_ref[pl.ds(2 * sites * c + 1, sites, stride=2), :]
            turned = jnp.concatenate(
                [cosine * real - sine * imag, sine * real + cosine * imag], axis=1
            )
            high, low = split(turned)
            rh[c * sites:(c + 1) * sites, :] = high
            rl[c * sites:(c + 1) * sites, :] = low
        tn = (((0,), (0,)), ((), ()))
        got = dot3((lh[...], ll[...]), (rh[...], rl[...]), tn)
        both = (
            got[:128, :128] + got[128:, 128:],
            got[:128, 128:] - got[128:, :128],
        )
        for half in range(2):
            for u in range(2):
                for p in range(2):
                    start = half * 64 + u * 32
                    part[m, half, u, p] = both[p][start:start + 32]

    steps = {}

    def step1(m):
        steps[m, 1] = remote(
            part.at[m, 1 - core], r1.at[m], send_sem.at[m, 0], recv_sem.at[m, 0], "slab", sibling
        )
        steps[m, 1].start()

    def step2(m):
        steps[m, 1].wait_recv()
        part[m, core] = part[m, core] + r1[m]
        steps[m, 2] = remote(
            part.at[m, core, 1 - sub], r2.at[m], send_sem.at[m, 1], recv_sem.at[m, 1], "slab", near
        )
        steps[m, 2].start()

    def step3(m):
        steps[m, 2].wait_recv()
        h2[m] = part[m, core, sub] + r2[m]
        steps[m, 3] = remote(h2.at[m], r3.at[m], send_sem.at[m, 2], recv_sem.at[m, 2], "slab", far)
        steps[m, 3].start()

    def step4(m):
        steps[m, 3].wait_recv()
        e_ref[m, core, time, sub] = (h2[m] + r3[m]) * scale
        done = e_ref.at[m, core, time, sub]
        steps[m, 4] = remote(done, done, send_sem.at[m, 3], recv_sem.at[m, 3], "slab", near)
        steps[m, 4].start()

    def step5(m):
        steps[m, 4].wait_recv()
        done = e_ref.at[m, core, time]
        for n, peer in enumerate(tm_peers):
            steps[m, 5, n] = remote(
                done, done, send_sem.at[m, 4 + n], recv_sem.at[m, 4 + n], "tm", peer
            )
            steps[m, 5, n].start()

    def step6(m):
        for n in range(len(tm_peers)):
            steps[m, 5, n].wait_recv()
        done = e_ref.at[m, core]
        steps[m, 6] = remote(done, done, send_sem.at[m, 7], recv_sem.at[m, 7], "slab", sibling)
        steps[m, 6].start()

    def step7(m):
        steps[m, 6].wait_recv()

    stages = (step1, step2, step3, step4, step5, step6, step7)
    for tick in range(moms + len(stages) - 1):
        if tick < moms:
            compute(tick)
        if tick == moms:
            p_far.wait_recv()
            d_ref[core] = psend[...] - precv[...]
            p_core.start()
        for m in range(moms):
            if 0 <= tick - m < len(stages):
                stages[tick - m](m)

    p_core.wait_recv()
    p_far.wait_send()
    p_core.wait_send()
    for copy in steps.values():
        copy.wait_send()


def dress_kernel(pairs_ref, e_ref, d_ref, out_ref):
    core = lax.axis_index("slab") % 2
    moms = e_ref.shape[0]
    pairs = d_ref.shape[1]
    block = d_ref.shape[3]
    for k in range(pairs):
        t1 = pairs_ref[k, 0]
        t2 = pairs_ref[k, 1]
        source = jnp.concatenate(
            [
                jnp.concatenate(
                    [e_ref[m, core, t1, :, 0].reshape(64, 128), e_ref[m, core, t1, :, 1].reshape(64, 128)],
                    axis=1,
                )
                for m in range(moms)
            ],
            axis=0,
        )
        peram_re = d_ref[:, k, 0].reshape(2 * block, 256)
        peram_im = d_ref[:, k, 1].reshape(2 * block, 256)
        (rh, rl), (ih, il) = split(peram_re), split(peram_im)

        def wide(re, im):
            return jnp.concatenate(
                [jnp.concatenate([re, im], axis=1), jnp.concatenate([im, -re], axis=1)], axis=0
            )

        fold = dot3(split(source), (wide(rh, ih), wide(rl, il)), NN)
        for m in range(moms):
            mine = fold[64 * m:64 * (m + 1)]
            left = jnp.concatenate(
                [
                    jnp.concatenate([mine[:, 0:128], mine[:, 256:384]], axis=1),
                    jnp.concatenate([mine[:, 128:256], mine[:, 384:512]], axis=1),
                ],
                axis=0,
            )
            sink_re = jnp.concatenate(
                [e_ref[m, h, t2, :, 0].reshape(64, 128) for h in range(2)], axis=0
            )
            sink_im = jnp.concatenate(
                [e_ref[m, h, t2, :, 1].reshape(64, 128) for h in range(2)], axis=0
            )
            (sh, sl), (th, tl) = split(sink_re), split(sink_im)

            def tall(re, im):
                return jnp.concatenate(
                    [jnp.concatenate([re, -im], axis=1), jnp.concatenate([im, re], axis=1)], axis=0
                )

            got = dot3(split(left), (tall(sh, th), tall(sl, tl)), NT)
            for t in range(4):
                for p in range(2):
                    out_ref[pl.ds(((k * moms + m) * 4 + t) * 2 + p, 64, stride=8 * moms * pairs), :] = got[
                        64 * (t % 2):64 * (t % 2 + 1), 128 * p:128 * (p + 1)
                    ]


def kernel_shards(eigvecs, perambulator, time_pairs, momenta):
    _, colours, sites, _, vecs = eigvecs.shape
    cols, pairs, _, order = perambulator.shape
    moms = momenta.shape[0]
    scale = 1.0 / math.sqrt(2.0 * colours * sites * SLABS)
    eig_rows = eigvecs.reshape(colours * sites * 2, vecs)
    per_rows = (
        perambulator.reshape(cols, pairs, 2, 4, vecs)
        .transpose(0, 1, 3, 2, 4)
        .reshape(cols * pairs * 8, vecs)
    )
    vmem = pl.BlockSpec(memory_space=pltpu.VMEM)
    smem = pl.BlockSpec(memory_space=pltpu.SMEM)
    depth = colours * sites
    elems, dress = pl.pallas_call(
        functools.partial(gather_kernel, scale),
        out_shape=(
            jax.ShapeDtypeStruct((moms, 2, TIMES, 2, 2, 32, vecs), F32),
            jax.ShapeDtypeStruct((2, pairs, 2, cols, 2 * vecs), F32),
        ),
        in_specs=[smem, vmem, vmem],
        out_specs=(vmem, vmem),
        scratch_shapes=[
            pltpu.VMEM((depth, 2 * vecs), BF16),
            pltpu.VMEM((depth, 2 * vecs), BF16),
            pltpu.VMEM((depth, 2 * vecs), BF16),
            pltpu.VMEM((depth, 2 * vecs), BF16),
            pltpu.VMEM((sites, 128), F32),
            pltpu.VMEM((moms, 2, 2, 2, 32, vecs), F32),
            pltpu.VMEM((moms, 2, 2, 32, vecs), F32),
            pltpu.VMEM((moms, 2, 32, vecs), F32),
            pltpu.VMEM((moms, 2, 32, vecs), F32),
            pltpu.VMEM((moms, 2, 32, vecs), F32),
            pltpu.VMEM((pairs, 2, cols, 2 * vecs), F32),
            pltpu.VMEM((pairs, 2, cols, 2 * vecs), F32),
            pltpu.SemaphoreType.DMA((moms, 8)),
            pltpu.SemaphoreType.DMA((moms, 8)),
            pltpu.SemaphoreType.DMA((2,)),
            pltpu.SemaphoreType.DMA((2,)),
        ],
        compiler_params=pltpu.CompilerParams(
            collective_id=0, has_side_effects=True, vmem_limit_bytes=40 * 2**20
        ),
        name="elementals",
    )(momenta, eig_rows, per_rows)
    rows = pl.pallas_call(
        dress_kernel,
        out_shape=jax.ShapeDtypeStruct((cols * pairs * moms * 8, vecs), F32),
        in_specs=[smem, vmem, vmem],
        out_specs=vmem,
        compiler_params=pltpu.CompilerParams(vmem_limit_bytes=40 * 2**20),
        name="dressing",
    )(time_pairs, elems, dress)
    return (
        rows.reshape(cols, pairs, moms, 4, 2, vecs)
        .transpose(0, 1, 2, 4, 3, 5)
        .reshape(cols, pairs, moms, 2, order)
    )


PRECISE = lax.Precision.HIGHEST
SPIN_MIX = ((1.0, 0.0, 1.0, 0.0), (0.0, 1.0, 0.0, 1.0), (1.0, 0.0, 1.0, 0.0), (0.0, 1.0, 0.0, 1.0))
CHIRAL = (1.0, 1.0, -1.0, -1.0)


def spin_tables():
    spin_mix = jnp.array(SPIN_MIX, jnp.float32)
    chiral = jnp.array(CHIRAL, jnp.float32)
    spin_dressed = chiral[:, None] * spin_mix * chiral[None, :]
    return (spin_mix, spin_dressed)


def phase_tables(momenta, site_ids):
    coords = jnp.stack([site_ids % LS, site_ids // LS % LS, site_ids // (LS * LS)])
    phase_turns = jnp.mod(jnp.sum(momenta[:, :, None] * coords[None, :, :], axis=1), LS)
    phase_angle = phase_turns.astype(jnp.float32) * (2.0 * math.pi / LS)
    return (jnp.cos(phase_angle), jnp.sin(phase_angle))


def elemental_terms(vectors, cosine_tab, sine_tab):
    local_times = vectors.shape[0]
    vec_count = vectors.shape[4]
    real_part = vectors[:, :, :, 0, :]
    imag_part = vectors[:, :, :, 1, :]
    left_rows = vectors.reshape(local_times, -1, vec_count)
    per_moment = []
    for mom_index in range(cosine_tab.shape[0]):
        cos_here = cosine_tab[mom_index][None, None, :, None]
        sin_here = sine_tab[mom_index][None, None, :, None]
        turned_re = cos_here * real_part - sin_here * imag_part
        turned_im = sin_here * real_part + cos_here * imag_part
        first_half = jnp.stack([turned_re, turned_im], axis=3).reshape(local_times, -1, vec_count)
        second_half = jnp.stack([turned_im, -turned_re], axis=3).reshape(local_times, -1, vec_count)
        right_cols = jnp.concatenate([first_half, second_half], axis=2)
        product = jnp.einsum("tki,tkj->tij", left_rows, right_cols, precision=PRECISE)
        per_moment.append(
            product.reshape(local_times, vec_count, 2, vec_count).transpose(0, 2, 1, 3)
        )
    return jnp.stack(per_moment, axis=1)


def shards(eigvecs, perambulator, time_pairs, momenta):
    colour_count = eigvecs.shape[1]
    site_count = eigvecs.shape[2]
    vec_count = eigvecs.shape[4]
    slab_count = lax.axis_size("slab")
    site_ids = lax.axis_index("slab") * site_count + jnp.arange(site_count, dtype=jnp.int32)
    cosine_tab, sine_tab = phase_tables(momenta, site_ids)
    partial_sums = elemental_terms(eigvecs, cosine_tab, sine_tab)
    summed = lax.psum(partial_sums, "slab")
    all_times = lax.all_gather(summed, "tm", axis=0, tiled=True)
    all_times = all_times * (1.0 / math.sqrt(2.0 * colour_count * site_count * slab_count))
    sink_elem = jnp.take(all_times, time_pairs[:, 1], axis=0)
    source_elem = jnp.take(all_times, time_pairs[:, 0], axis=0)
    sink_re = sink_elem[:, :, 0]
    sink_im = sink_elem[:, :, 1]
    spin_mix, spin_dressed = spin_tables()
    panel_cols = perambulator.shape[0]
    pair_count = perambulator.shape[1]
    spin_order = perambulator.shape[3]
    spin_count = spin_order // vec_count
    mom_count = momenta.shape[0]
    panel_start = lax.axis_index("slab") * panel_cols
    panel_spin = panel_start // vec_count
    panel_vec = panel_start % vec_count
    chiral_col = lax.dynamic_index_in_dim(spin_dressed, panel_spin, 1, keepdims=False)
    source_block = lax.dynamic_slice_in_dim(source_elem, panel_vec, panel_cols, 3)
    dress_re = jnp.einsum("s,kmbi->kmsib", chiral_col, source_block[:, :, 0]).reshape(
        pair_count, mom_count, spin_order, panel_cols
    )
    dress_im = -jnp.einsum("s,kmbi->kmsib", chiral_col, source_block[:, :, 1]).reshape(
        pair_count, mom_count, spin_order, panel_cols
    )
    peram_piece = lax.all_gather(perambulator, "slab", axis=0, tiled=True)
    piece_re = peram_piece[:, :, 0]
    piece_im = peram_piece[:, :, 1]
    fold_re = jnp.einsum("ckr,kmcb->bkmr", piece_re, dress_re, precision=PRECISE) - jnp.einsum(
        "ckr,kmcb->bkmr", piece_im, dress_im, precision=PRECISE
    )
    fold_im = jnp.einsum("ckr,kmcb->bkmr", piece_re, dress_im, precision=PRECISE) + jnp.einsum(
        "ckr,kmcb->bkmr", piece_im, dress_re, precision=PRECISE
    )
    fold_re, fold_im = (fold_re, fold_im)
    fold_re = fold_re.reshape(panel_cols, pair_count, mom_count, spin_count, vec_count)
    fold_im = fold_im.reshape(panel_cols, pair_count, mom_count, spin_count, vec_count)
    mixed_re = jnp.einsum("bkmsj,kmij->bkmsi", fold_re, sink_re, precision=PRECISE) - jnp.einsum(
        "bkmsj,kmij->bkmsi", fold_im, sink_im, precision=PRECISE
    )
    mixed_im = jnp.einsum("bkmsj,kmij->bkmsi", fold_re, sink_im, precision=PRECISE) + jnp.einsum(
        "bkmsj,kmij->bkmsi", fold_im, sink_re, precision=PRECISE
    )
    final_re = jnp.einsum("ts,bkmsi->bkmti", spin_mix, mixed_re, precision=PRECISE).reshape(
        panel_cols, pair_count, mom_count, spin_order
    )
    final_im = jnp.einsum("ts,bkmsi->bkmti", spin_mix, mixed_im, precision=PRECISE).reshape(
        panel_cols, pair_count, mom_count, spin_order
    )
    dressed = jnp.stack([final_re, final_im], axis=3)
    return dressed


def solution(mesh):
    known = mesh.shape["tm"] == TIMES and mesh.shape["slab"] == SLABS
    return jax.shard_map(
        kernel_shards if known else shards,
        mesh=mesh,
        in_specs=(
            P("tm", None, "slab", None, None),
            P("slab", "tm", None, None),
            P("tm", None),
            P(),
        ),
        out_specs=P("slab", "tm", None, None, None),
        check_vma=False,
    )
```

```python
import functools
import math

import jax
import jax.numpy as jnp
from jax import lax
from jax.experimental import pallas as pl
from jax.experimental.pallas import tpu as pltpu
from jax.sharding import PartitionSpec as P

LS = 48
SLABS = 8
TIMES = 4
BF16 = jnp.bfloat16
F32 = jnp.float32
NN = (((1,), (0,)), ((), ()))
NT = (((1,), (1,)), ((), ()))


def split(value):
    high = value.astype(BF16)
    return high, (value - high.astype(F32)).astype(BF16)


def dot3(left, right, dims):
    def one(x, y):
        return lax.dot_general(x, y, dims, preferred_element_type=F32)

    return one(left[0], right[0]) + (one(left[0], right[1]) + one(left[1], right[0]))


def floor_div(value, by):
    return jnp.floor((value + 0.5) * (1.0 / by))


def correlator_kernel(
    scale, mom_hbm, eig_hbm, per_hbm, pairs_hbm, out_hbm,
    e_refs, d_ref, out_ref, out_sem, pairs_ref, mom_ref, eig_ref, per_ref, load_sem, left, rh, rl, phase, part, r1, r2, h2, r3, psend, precv,
    send_sem, recv_sem, psend_sem, precv_sem,
):
    slab = lax.axis_index("slab")
    time = lax.axis_index("tm")
    core = slab % 2
    sub = (slab // 2) % 2
    sibling = slab + 1 - 2 * core
    near = slab + 2 - 4 * sub
    far = (slab + 4) % SLABS
    tm_peers = (time + 1 - 2 * (time % 2), (time + 2) % TIMES, TIMES - 1 - time)
    slab_peers = (sibling, near, far)

    loads = [
        pltpu.make_async_copy(src, dst, load_sem.at[n])
        for n, (src, dst) in enumerate(
            ((per_hbm, per_ref), (mom_hbm, mom_ref), (eig_hbm, eig_ref), (pairs_hbm, pairs_ref))
        )
    ]
    for load in loads:
        load.start()

    barrier = pltpu.get_barrier_semaphore()
    for peer in slab_peers:
        pl.semaphore_signal(barrier, inc=1, device_id={"slab": peer}, device_id_type=pl.DeviceIdType.MESH)
    for peer in tm_peers:
        pl.semaphore_signal(barrier, inc=1, device_id={"tm": peer}, device_id_type=pl.DeviceIdType.MESH)

    loads[0].wait()
    pairs = psend.shape[0]
    cols = psend.shape[2]
    for k in range(pairs):
        for p in range(2):
            spins = [
                per_ref[pl.ds(k * 8 + t * 2 + p, cols, stride=8 * pairs), :] for t in range(4)
            ]
            psend[k, p, :, 0:128] = spins[0] + spins[2]
            psend[k, p, :, 128:256] = spins[1] + spins[3]

    pl.semaphore_wait(barrier, len(slab_peers) + len(tm_peers))

    def remote(src, dst, ssem, rsem, axis, peer):
        return pltpu.make_async_remote_copy(
            src_ref=src, dst_ref=dst, send_sem=ssem, recv_sem=rsem,
            device_id={axis: peer}, device_id_type=pl.DeviceIdType.MESH,
        )

    p_far = [
        remote(psend.at[k], precv.at[k], psend_sem.at[0, k], precv_sem.at[0, k], "slab", far)
        for k in range(pairs)
    ]
    p_core = [
        remote(d_ref.at[core, k], d_ref.at[core, k], psend_sem.at[1, k], precv_sem.at[1, k], "slab", sibling)
        for k in range(pairs)
    ]

    def difference(k):
        p_far[k].wait_recv()
        d_ref[core, k] = psend[k] - precv[k]
        p_core[k].start()

    p_far[0].start()
    loads[1].wait()

    moms = mom_ref.shape[0]
    sites = phase.shape[0]
    site = (lax.broadcasted_iota(jnp.int32, (sites, 128), 0) + slab * sites).astype(F32)
    lane = lax.broadcasted_iota(jnp.int32, (sites, 128), 1)
    row = floor_div(site, LS)
    plane = floor_div(row, LS)
    coords = (site - LS * row, row - LS * plane, plane)
    turns = jnp.zeros((sites, 128), F32)
    for m in range(moms):
        mine = mom_ref[m, 0].astype(F32) * coords[0]
        mine = mine + mom_ref[m, 1].astype(F32) * coords[1]
        mine = mine + mom_ref[m, 2].astype(F32) * coords[2]
        turns = jnp.where(lane % moms == m, mine, turns)
    turns = turns - LS * floor_div(turns, LS)
    turns = jnp.where(lane >= moms, turns - LS / 4, turns)
    phase[...] = jnp.cos(turns * (2.0 * math.pi / LS))

    loads[2].wait()
    rows = []
    colours = eig_ref.shape[0] // (2 * sites)
    for c in range(colours):
        real = eig_ref[pl.ds(2 * sites * c, sites, stride=2), :]
        imag = eig_ref[pl.ds(2 * sites * c + 1, sites, stride=2), :]
        rows.append(jnp.concatenate([real, imag], axis=1))
    high, low = split(jnp.concatenate(rows, axis=0).T)
    wide = rows[0].shape[1]
    left[:wide] = high
    left[wide:] = low

    def compute(m):
        cosine = phase[:, m:m + 1]
        sine = phase[:, moms + m:moms + m + 1]
        for c in range(colours):
            real = eig_ref[pl.ds(2 * sites * c, sites, stride=2), :]
            imag = eig_ref[pl.ds(2 * sites * c + 1, sites, stride=2), :]
            turned = jnp.concatenate(
                [cosine * real - sine * imag, sine * real + cosine * imag], axis=1
            )
            high, low = split(turned)
            rh[c * sites:(c + 1) * sites, :] = high
            rl[c * sites:(c + 1) * sites, :] = low
        coarse = lax.dot_general(left[...], rh[...], NN, preferred_element_type=F32)
        fine = lax.dot_general(left[:wide], rl[...], NN, preferred_element_type=F32)
        got = coarse[:wide] + (coarse[wide:] + fine)
        both = (
            got[:128, :128] + got[128:, 128:],
            got[:128, 128:] - got[128:, :128],
        )
        for half in range(2):
            for u in range(2):
                for p in range(2):
                    start = half * 64 + u * 32
                    part[m, half, u, p] = both[p][start:start + 32]

    steps = {}

    def step1(m):
        steps[m, 1] = remote(
            part.at[m, 1 - core], r1.at[m], send_sem.at[m, 0], recv_sem.at[m, 0], "slab", sibling
        )
        steps[m, 1].start()

    def step2(m):
        steps[m, 1].wait_recv()
        part[m, core] = part[m, core] + r1[m]
        steps[m, 2] = remote(
            part.at[m, core, 1 - sub], r2.at[m], send_sem.at[m, 1], recv_sem.at[m, 1], "slab", near
        )
        steps[m, 2].start()

    def step3(m):
        steps[m, 2].wait_recv()
        h2[m] = part[m, core, sub] + r2[m]
        steps[m, 3] = remote(h2.at[m], r3.at[m], send_sem.at[m, 2], recv_sem.at[m, 2], "slab", far)
        steps[m, 3].start()

    def step4(m):
        steps[m, 3].wait_recv()
        e_refs[m][core, time, sub] = (h2[m] + r3[m]) * scale
        done = e_refs[m].at[core, time, sub]
        steps[m, 4] = remote(done, done, send_sem.at[m, 3], recv_sem.at[m, 3], "slab", near)
        steps[m, 4].start()

    def step5(m):
        steps[m, 4].wait_recv()
        done = e_refs[m].at[core, time]
        for n, peer in enumerate(tm_peers):
            steps[m, 5, n] = remote(
                done, done, send_sem.at[m, 4 + n], recv_sem.at[m, 4 + n], "tm", peer
            )
            steps[m, 5, n].start()

    def step6(m):
        for n in range(len(tm_peers)):
            steps[m, 5, n].wait_recv()
        done = e_refs[m].at[core]
        steps[m, 6] = remote(done, done, send_sem.at[m, 7], recv_sem.at[m, 7], "slab", sibling)
        steps[m, 6].start()

    def step7(m):
        steps[m, 6].wait_recv()
        if m == 0:
            for copy in p_core:
                copy.wait_recv()
            loads[3].wait()
        for k in range(pairs):
            dress(m, k)
        rows = cols * pairs * 8
        stores[m] = pltpu.make_async_copy(
            out_ref.at[pl.ds(m * rows, rows)].reshape(cols, pairs, 8, 128),
            out_hbm.at[:, :, m],
            out_sem.at[m],
        )
        stores[m].start()

    def dress(m, k):
        e_ref = e_refs[m]
        t1 = pairs_ref[k, 0]
        t2 = pairs_ref[k, 1]

        def block(half, t, p):
            return e_ref[half, t, :, p].reshape(64, 128)

        source = split(jnp.concatenate([block(core, t1, 0), block(core, t1, 1)], axis=1))
        re_high, re_low = split(d_ref[:, k, 0].reshape(2 * cols, 256))
        im_high, im_low = split(d_ref[:, k, 1].reshape(2 * cols, 256))

        def wide_of(re, im):
            return jnp.concatenate(
                [jnp.concatenate([re, im], axis=1), jnp.concatenate([im, -re], axis=1)], axis=0
            )

        fold = dot3(source, (wide_of(re_high, im_high), wide_of(re_low, im_low)), NN)
        spun = jnp.concatenate(
            [
                jnp.concatenate([fold[:, 0:128], fold[:, 256:384]], axis=1),
                jnp.concatenate([fold[:, 128:256], fold[:, 384:512]], axis=1),
            ],
            axis=0,
        )
        sink = [
            split(jnp.concatenate([block(0, t2, p), block(1, t2, p)], axis=0)) for p in range(2)
        ]

        def tall_of(re, im):
            return jnp.concatenate(
                [jnp.concatenate([re, -im], axis=1), jnp.concatenate([im, re], axis=1)], axis=0
            )

        right = tuple(tall_of(sink[0][n], sink[1][n]) for n in range(2))
        got = dot3(split(spun), right, NT)
        for t in range(4):
            for p in range(2):
                start = m * cols * pairs * 8 + k * 8 + t * 2 + p
                out_ref[pl.ds(start, cols, stride=8 * pairs), :] = got[
                    64 * (t % 2):64 * (t % 2 + 1), 128 * p:128 * (p + 1)
                ]

    stores = {}
    stages = (step1, step2, step3, step4, step5, step6, step7)
    for tick in range(moms + len(stages) - 1):
        if tick < moms:
            compute(tick)
        if tick == moms + 2:
            for k in range(1, pairs):
                difference(k)
        for m in range(moms):
            if 0 <= tick - m < len(stages):
                stages[tick - m](m)
        if tick == moms:
            for k in range(1, pairs):
                p_far[k].start()
            difference(0)

    for copy in p_far + p_core:
        copy.wait_send()
    for copy in steps.values():
        copy.wait_send()
    for store in stores.values():
        store.wait()


def kernel_shards(eigvecs, perambulator, time_pairs, momenta):
    _, colours, sites, _, vecs = eigvecs.shape
    cols, pairs, _, order = perambulator.shape
    moms = momenta.shape[0]
    scale = 1.0 / math.sqrt(2.0 * colours * sites * SLABS)
    eig_rows = eigvecs.reshape(colours * sites * 2, vecs)
    per_rows = (
        perambulator.reshape(cols, pairs, 2, 4, vecs)
        .transpose(0, 1, 3, 2, 4)
        .reshape(cols * pairs * 8, vecs)
    )
    hbm = pl.BlockSpec(memory_space=pltpu.HBM)
    depth = colours * sites
    rows = pl.pallas_call(
        functools.partial(correlator_kernel, scale),
        out_shape=jax.ShapeDtypeStruct((cols, pairs, moms, 8, vecs), F32),
        in_specs=[hbm, hbm, hbm, hbm],
        out_specs=hbm,
        scratch_shapes=[
            [pltpu.VMEM((2, TIMES, 2, 2, 32, vecs), F32) for _ in range(moms)],
            pltpu.VMEM((2, pairs, 2, cols, 2 * vecs), F32),
            pltpu.VMEM((moms * cols * pairs * 8, vecs), F32),
            pltpu.SemaphoreType.DMA((moms,)),
            pltpu.SMEM(time_pairs.shape, jnp.int32),
            pltpu.SMEM(momenta.shape, jnp.int32),
            pltpu.VMEM(eig_rows.shape, F32),
            pltpu.VMEM(per_rows.shape, F32),
            pltpu.SemaphoreType.DMA((4,)),
            pltpu.VMEM((4 * vecs, depth), BF16),
            pltpu.VMEM((depth, 2 * vecs), BF16),
            pltpu.VMEM((depth, 2 * vecs), BF16),
            pltpu.VMEM((sites, 128), F32),
            pltpu.VMEM((moms, 2, 2, 2, 32, vecs), F32),
            pltpu.VMEM((moms, 2, 2, 32, vecs), F32),
            pltpu.VMEM((moms, 2, 32, vecs), F32),
            pltpu.VMEM((moms, 2, 32, vecs), F32),
            pltpu.VMEM((moms, 2, 32, vecs), F32),
            pltpu.VMEM((pairs, 2, cols, 2 * vecs), F32),
            pltpu.VMEM((pairs, 2, cols, 2 * vecs), F32),
            pltpu.SemaphoreType.DMA((moms, 8)),
            pltpu.SemaphoreType.DMA((moms, 8)),
            pltpu.SemaphoreType.DMA((2, pairs)),
            pltpu.SemaphoreType.DMA((2, pairs)),
        ],
        compiler_params=pltpu.CompilerParams(
            collective_id=0, has_side_effects=True, vmem_limit_bytes=61 * 2**20
        ),
        name="correlators",
    )(momenta, eig_rows, per_rows, time_pairs)
    return (
        rows.reshape(cols, pairs, moms, 4, 2, vecs)
        .transpose(0, 1, 2, 4, 3, 5)
        .reshape(cols, pairs, moms, 2, order)
    )


PRECISE = lax.Precision.HIGHEST
SPIN_MIX = ((1.0, 0.0, 1.0, 0.0), (0.0, 1.0, 0.0, 1.0), (1.0, 0.0, 1.0, 0.0), (0.0, 1.0, 0.0, 1.0))
CHIRAL = (1.0, 1.0, -1.0, -1.0)


def spin_tables():
    spin_mix = jnp.array(SPIN_MIX, jnp.float32)
    chiral = jnp.array(CHIRAL, jnp.float32)
    spin_dressed = chiral[:, None] * spin_mix * chiral[None, :]
    return (spin_mix, spin_dressed)


def phase_tables(momenta, site_ids):
    coords = jnp.stack([site_ids % LS, site_ids // LS % LS, site_ids // (LS * LS)])
    phase_turns = jnp.mod(jnp.sum(momenta[:, :, None] * coords[None, :, :], axis=1), LS)
    phase_angle = phase_turns.astype(jnp.float32) * (2.0 * math.pi / LS)
    return (jnp.cos(phase_angle), jnp.sin(phase_angle))


def elemental_terms(vectors, cosine_tab, sine_tab):
    local_times = vectors.shape[0]
    vec_count = vectors.shape[4]
    real_part = vectors[:, :, :, 0, :]
    imag_part = vectors[:, :, :, 1, :]
    left_rows = vectors.reshape(local_times, -1, vec_count)
    per_moment = []
    for mom_index in range(cosine_tab.shape[0]):
        cos_here = cosine_tab[mom_index][None, None, :, None]
        sin_here = sine_tab[mom_index][None, None, :, None]
        turned_re = cos_here * real_part - sin_here * imag_part
        turned_im = sin_here * real_part + cos_here * imag_part
        first_half = jnp.stack([turned_re, turned_im], axis=3).reshape(local_times, -1, vec_count)
        second_half = jnp.stack([turned_im, -turned_re], axis=3).reshape(local_times, -1, vec_count)
        right_cols = jnp.concatenate([first_half, second_half], axis=2)
        product = jnp.einsum("tki,tkj->tij", left_rows, right_cols, precision=PRECISE)
        per_moment.append(
            product.reshape(local_times, vec_count, 2, vec_count).transpose(0, 2, 1, 3)
        )
    return jnp.stack(per_moment, axis=1)


def shards(eigvecs, perambulator, time_pairs, momenta):
    colour_count = eigvecs.shape[1]
    site_count = eigvecs.shape[2]
    vec_count = eigvecs.shape[4]
    slab_count = lax.axis_size("slab")
    site_ids = lax.axis_index("slab") * site_count + jnp.arange(site_count, dtype=jnp.int32)
    cosine_tab, sine_tab = phase_tables(momenta, site_ids)
    partial_sums = elemental_terms(eigvecs, cosine_tab, sine_tab)
    summed = lax.psum(partial_sums, "slab")
    all_times = lax.all_gather(summed, "tm", axis=0, tiled=True)
    all_times = all_times * (1.0 / math.sqrt(2.0 * colour_count * site_count * slab_count))
    sink_elem = jnp.take(all_times, time_pairs[:, 1], axis=0)
    source_elem = jnp.take(all_times, time_pairs[:, 0], axis=0)
    sink_re = sink_elem[:, :, 0]
    sink_im = sink_elem[:, :, 1]
    spin_mix, spin_dressed = spin_tables()
    panel_cols = perambulator.shape[0]
    pair_count = perambulator.shape[1]
    spin_order = perambulator.shape[3]
    spin_count = spin_order // vec_count
    mom_count = momenta.shape[0]
    panel_start = lax.axis_index("slab") * panel_cols
    panel_spin = panel_start // vec_count
    panel_vec = panel_start % vec_count
    chiral_col = lax.dynamic_index_in_dim(spin_dressed, panel_spin, 1, keepdims=False)
    source_block = lax.dynamic_slice_in_dim(source_elem, panel_vec, panel_cols, 3)
    dress_re = jnp.einsum("s,kmbi->kmsib", chiral_col, source_block[:, :, 0]).reshape(
        pair_count, mom_count, spin_order, panel_cols
    )
    dress_im = -jnp.einsum("s,kmbi->kmsib", chiral_col, source_block[:, :, 1]).reshape(
        pair_count, mom_count, spin_order, panel_cols
    )
    peram_piece = lax.all_gather(perambulator, "slab", axis=0, tiled=True)
    piece_re = peram_piece[:, :, 0]
    piece_im = peram_piece[:, :, 1]
    fold_re = jnp.einsum("ckr,kmcb->bkmr", piece_re, dress_re, precision=PRECISE) - jnp.einsum(
        "ckr,kmcb->bkmr", piece_im, dress_im, precision=PRECISE
    )
    fold_im = jnp.einsum("ckr,kmcb->bkmr", piece_re, dress_im, precision=PRECISE) + jnp.einsum(
        "ckr,kmcb->bkmr", piece_im, dress_re, precision=PRECISE
    )
    fold_re, fold_im = (fold_re, fold_im)
    fold_re = fold_re.reshape(panel_cols, pair_count, mom_count, spin_count, vec_count)
    fold_im = fold_im.reshape(panel_cols, pair_count, mom_count, spin_count, vec_count)
    mixed_re = jnp.einsum("bkmsj,kmij->bkmsi", fold_re, sink_re, precision=PRECISE) - jnp.einsum(
        "bkmsj,kmij->bkmsi", fold_im, sink_im, precision=PRECISE
    )
    mixed_im = jnp.einsum("bkmsj,kmij->bkmsi", fold_re, sink_im, precision=PRECISE) + jnp.einsum(
        "bkmsj,kmij->bkmsi", fold_im, sink_re, precision=PRECISE
    )
    final_re = jnp.einsum("ts,bkmsi->bkmti", spin_mix, mixed_re, precision=PRECISE).reshape(
        panel_cols, pair_count, mom_count, spin_order
    )
    final_im = jnp.einsum("ts,bkmsi->bkmti", spin_mix, mixed_im, precision=PRECISE).reshape(
        panel_cols, pair_count, mom_count, spin_order
    )
    dressed = jnp.stack([final_re, final_im], axis=3)
    return dressed


def solution(mesh):
    known = mesh.shape["tm"] == TIMES and mesh.shape["slab"] == SLABS
    return jax.shard_map(
        kernel_shards if known else shards,
        mesh=mesh,
        in_specs=(
            P("tm", None, "slab", None, None),
            P("slab", "tm", None, None),
            P("tm", None),
            P(),
        ),
        out_specs=P("slab", "tm", None, None, None),
        check_vma=False,
    )
```

```python
import functools
import math

import jax
import jax.numpy as jnp
from jax import lax
from jax.experimental import pallas as pl
from jax.experimental.pallas import tpu as pltpu
from jax.sharding import PartitionSpec as P

LS = 48
SLABS = 8
TIMES = 4
PARTS = 4
BF16 = jnp.bfloat16
F32 = jnp.float32
NN = (((1,), (0,)), ((), ()))
NT = (((1,), (1,)), ((), ()))


def split(value):
    high = value.astype(BF16)
    return high, (value - high.astype(F32)).astype(BF16)


def dot3(left, right, dims):
    def one(x, y):
        return lax.dot_general(x, y, dims, preferred_element_type=F32)

    return one(left[0], right[0]) + (one(left[0], right[1]) + one(left[1], right[0]))


def floor_div(value, by):
    return jnp.floor((value + 0.5) * (1.0 / by))


def correlator_kernel(
    scale, mom_hbm, eig_hbm, per_hbm, pairs_hbm, out_hbm,
    e_refs, d_ref, out_ref, out_sem, pairs_ref, mom_ref, eig_ref, per_ref, load_sem, left, rh, rl, phase, part, r1, h2, r3, psend, precv,
    send_sem, recv_sem, psend_sem, precv_sem,
):
    slab = lax.axis_index("slab")
    time = lax.axis_index("tm")
    core = slab % 2
    sub = (slab // 2) % 2
    sibling = slab + 1 - 2 * core
    near = slab + 2 - 4 * sub
    cross = near + 1 - 2 * core
    far = (slab + 4) % SLABS
    tm_peers = (time + 1 - 2 * (time % 2), (time + 2) % TIMES, TIMES - 1 - time)
    slab_peers = (sibling, near, cross, far)

    loads = [
        pltpu.make_async_copy(src, dst, load_sem.at[n])
        for n, (src, dst) in enumerate(
            ((per_hbm, per_ref), (mom_hbm, mom_ref), (eig_hbm, eig_ref), (pairs_hbm, pairs_ref))
        )
    ]
    for load in loads:
        load.start()

    barrier = pltpu.get_barrier_semaphore()
    for peer in slab_peers:
        pl.semaphore_signal(barrier, inc=1, device_id={"slab": peer}, device_id_type=pl.DeviceIdType.MESH)
    for peer in tm_peers:
        pl.semaphore_signal(barrier, inc=1, device_id={"tm": peer}, device_id_type=pl.DeviceIdType.MESH)

    loads[0].wait()
    pairs = psend.shape[0]
    cols = psend.shape[2]
    for k in range(pairs):
        for p in range(2):
            spins = [
                per_ref[pl.ds(k * 8 + t * 2 + p, cols, stride=8 * pairs), :] for t in range(4)
            ]
            psend[k, p, :, 0:128] = spins[0] + spins[2]
            psend[k, p, :, 128:256] = spins[1] + spins[3]

    pl.semaphore_wait(barrier, len(slab_peers) + len(tm_peers))

    def remote(src, dst, ssem, rsem, axis, peer):
        return pltpu.make_async_remote_copy(
            src_ref=src, dst_ref=dst, send_sem=ssem, recv_sem=rsem,
            device_id={axis: peer}, device_id_type=pl.DeviceIdType.MESH,
        )

    p_far = [
        remote(psend.at[k], precv.at[k], psend_sem.at[0, k], precv_sem.at[0, k], "slab", far)
        for k in range(pairs)
    ]
    p_core = [
        remote(d_ref.at[core, k], d_ref.at[core, k], psend_sem.at[1, k], precv_sem.at[1, k], "slab", sibling)
        for k in range(pairs)
    ]

    def difference(k):
        p_far[k].wait_recv()
        d_ref[core, k] = psend[k] - precv[k]
        p_core[k].start()

    p_far[0].start()
    loads[1].wait()

    moms = mom_ref.shape[0]
    sites = phase.shape[0]
    site = (lax.broadcasted_iota(jnp.int32, (sites, 128), 0) + slab * sites).astype(F32)
    lane = lax.broadcasted_iota(jnp.int32, (sites, 128), 1)
    row = floor_div(site, LS)
    plane = floor_div(row, LS)
    coords = (site - LS * row, row - LS * plane, plane)
    turns = jnp.zeros((sites, 128), F32)
    for m in range(moms):
        mine = mom_ref[m, 0].astype(F32) * coords[0]
        mine = mine + mom_ref[m, 1].astype(F32) * coords[1]
        mine = mine + mom_ref[m, 2].astype(F32) * coords[2]
        turns = jnp.where(lane % moms == m, mine, turns)
    turns = turns - LS * floor_div(turns, LS)
    turns = jnp.where(lane >= moms, turns - LS / 4, turns)
    phase[...] = jnp.cos(turns * (2.0 * math.pi / LS))

    loads[2].wait()
    rows = []
    colours = eig_ref.shape[0] // (2 * sites)
    for c in range(colours):
        real = eig_ref[pl.ds(2 * sites * c, sites, stride=2), :]
        imag = eig_ref[pl.ds(2 * sites * c + 1, sites, stride=2), :]
        rows.append(jnp.concatenate([real, imag], axis=1))
    high, low = split(jnp.concatenate(rows, axis=0).T)
    wide = rows[0].shape[1]
    left[:wide] = high
    left[wide:] = low

    def compute(m):
        cosine = phase[:, m:m + 1]
        sine = phase[:, moms + m:moms + m + 1]
        for c in range(colours):
            real = eig_ref[pl.ds(2 * sites * c, sites, stride=2), :]
            imag = eig_ref[pl.ds(2 * sites * c + 1, sites, stride=2), :]
            turned = jnp.concatenate(
                [cosine * real - sine * imag, sine * real + cosine * imag], axis=1
            )
            high, low = split(turned)
            rh[c * sites:(c + 1) * sites, :] = high
            rl[c * sites:(c + 1) * sites, :] = low
        coarse = lax.dot_general(left[...], rh[...], NN, preferred_element_type=F32)
        fine = lax.dot_general(left[:wide], rl[...], NN, preferred_element_type=F32)
        got = coarse[:wide] + (coarse[wide:] + fine)
        both = (
            got[:128, :128] + got[128:, 128:],
            got[:128, 128:] - got[128:, :128],
        )
        for half in range(2):
            for u in range(2):
                for p in range(2):
                    start = half * 64 + u * 32
                    part[m, half, u, p] = both[p][start:start + 32]

    steps = {}

    def step1(m):
        for n, (half, u, peer) in enumerate(
            ((1 - core, sub, sibling), (core, 1 - sub, near), (1 - core, 1 - sub, cross))
        ):
            steps[m, 1, n] = remote(
                part.at[m, half, u], r1.at[m, n], send_sem.at[m, n], recv_sem.at[m, n], "slab", peer
            )
            steps[m, 1, n].start()

    def step2(m):
        for n in range(3):
            steps[m, 1, n].wait_recv()
        h2[m] = (part[m, core, sub] + r1[m, 0]) + (r1[m, 1] + r1[m, 2])
        steps[m, 2] = remote(h2.at[m], r3.at[m], send_sem.at[m, 3], recv_sem.at[m, 3], "slab", far)
        steps[m, 2].start()

    def step3(m):
        steps[m, 2].wait_recv()
        e_refs[m][core, time, sub] = (h2[m] + r3[m]) * scale
        done = e_refs[m].at[core, time, sub]
        steps[m, 3] = remote(done, done, send_sem.at[m, 4], recv_sem.at[m, 4], "slab", near)
        steps[m, 3].start()

    def step4(m):
        steps[m, 3].wait_recv()
        done = e_refs[m].at[core, time]
        for n, peer in enumerate(tm_peers):
            steps[m, 4, n] = remote(
                done, done, send_sem.at[m, 5 + n], recv_sem.at[m, 5 + n], "tm", peer
            )
            steps[m, 4, n].start()

    def step5(m):
        for n in range(len(tm_peers)):
            steps[m, 4, n].wait_recv()
        done = e_refs[m].at[core]
        steps[m, 5] = remote(done, done, send_sem.at[m, 8], recv_sem.at[m, 8], "slab", sibling)
        steps[m, 5].start()

    def step6(m):
        steps[m, 5].wait_recv()
        if m == 0:
            p_core[0].wait_recv()
            loads[3].wait()
        dress(m, 0)

    rows_each = cols * 8

    def dress(m, k):
        e_ref = e_refs[m]
        t1 = pairs_ref[k, 0]
        t2 = pairs_ref[k, 1]

        def block(half, t, p):
            return e_ref[half, t, :, p].reshape(64, 128)

        source = split(jnp.concatenate([block(core, t1, 0), block(core, t1, 1)], axis=1))
        re_high, re_low = split(d_ref[:, k, 0].reshape(2 * cols, 256))
        im_high, im_low = split(d_ref[:, k, 1].reshape(2 * cols, 256))

        def wide_of(re, im):
            return jnp.concatenate(
                [jnp.concatenate([re, im], axis=1), jnp.concatenate([im, -re], axis=1)], axis=0
            )

        fold = dot3(source, (wide_of(re_high, im_high), wide_of(re_low, im_low)), NN)
        spun = jnp.concatenate(
            [
                jnp.concatenate([fold[:, 0:128], fold[:, 256:384]], axis=1),
                jnp.concatenate([fold[:, 128:256], fold[:, 384:512]], axis=1),
            ],
            axis=0,
        )
        sink = [
            split(jnp.concatenate([block(0, t2, p), block(1, t2, p)], axis=0)) for p in range(2)
        ]

        def tall_of(re, im):
            return jnp.concatenate(
                [jnp.concatenate([re, -im], axis=1), jnp.concatenate([im, re], axis=1)], axis=0
            )

        right = tuple(tall_of(sink[0][n], sink[1][n]) for n in range(2))
        got = dot3(split(spun), right, NT)
        for t in range(4):
            for p in range(2):
                start = (m * pairs + k) * rows_each + t * 2 + p
                out_ref[pl.ds(start, cols, stride=8), :] = got[
                    64 * (t % 2):64 * (t % 2 + 1), 128 * p:128 * (p + 1)
                ]
        stores[m, k] = pltpu.make_async_copy(
            out_ref.at[pl.ds((m * pairs + k) * rows_each, rows_each)].reshape(cols, 8, 128),
            out_hbm.at[:, k, m],
            out_sem.at[m, k],
        )
        stores[m, k].start()

    stores = {}
    stages = (step1, step2, step3, step4, step5, step6)
    ticks = moms + len(stages) - 1
    for tick in range(ticks):
        if tick < moms:
            compute(tick)
        if tick == ticks - 1:
            for k in range(1, pairs):
                difference(k)
        for m in range(moms):
            if 0 <= tick - m < len(stages):
                stages[tick - m](m)
        if tick == moms - 1:
            for k in range(1, pairs):
                p_far[k].start()
        if tick == moms:
            difference(0)
    for k in range(1, pairs):
        p_core[k].wait_recv()
        for m in range(moms):
            dress(m, k)

    for copy in p_far + p_core:
        copy.wait_send()
    for copy in steps.values():
        copy.wait_send()
    for store in stores.values():
        store.wait()


def copy_kernel(src, dst, sem):
    share = src.shape[0] // PARTS
    copies = [
        pltpu.make_async_copy(
            src.at[pl.ds(n * share, share)], dst.at[pl.ds(n * share, share)], sem.at[n]
        )
        for n in range(PARTS)
    ]
    for copy in copies:
        copy.start()
    for copy in copies:
        copy.wait()


def kernel_shards(eigvecs, perambulator, time_pairs, momenta):
    _, colours, sites, _, vecs = eigvecs.shape
    cols, pairs, _, order = perambulator.shape
    moms = momenta.shape[0]
    scale = 1.0 / math.sqrt(2.0 * colours * sites * SLABS)
    eig_rows = eigvecs.reshape(colours * sites * 2, vecs)
    per_rows = (
        perambulator.reshape(cols, pairs, 2, 4, vecs)
        .transpose(0, 1, 3, 2, 4)
        .reshape(cols * pairs * 8, vecs)
    )
    hbm = pl.BlockSpec(memory_space=pltpu.HBM)
    depth = colours * sites
    rows = pl.pallas_call(
        functools.partial(correlator_kernel, scale),
        out_shape=jax.ShapeDtypeStruct((cols, pairs, moms, 8, vecs), F32),
        in_specs=[hbm, hbm, hbm, hbm],
        out_specs=hbm,
        scratch_shapes=[
            [pltpu.VMEM((2, TIMES, 2, 2, 32, vecs), F32) for _ in range(moms)],
            pltpu.VMEM((2, pairs, 2, cols, 2 * vecs), F32),
            pltpu.VMEM((moms * cols * pairs * 8, vecs), F32),
            pltpu.SemaphoreType.DMA((moms, pairs)),
            pltpu.SMEM(time_pairs.shape, jnp.int32),
            pltpu.SMEM(momenta.shape, jnp.int32),
            pltpu.VMEM(eig_rows.shape, F32),
            pltpu.VMEM(per_rows.shape, F32),
            pltpu.SemaphoreType.DMA((4,)),
            pltpu.VMEM((4 * vecs, depth), BF16),
            pltpu.VMEM((depth, 2 * vecs), BF16),
            pltpu.VMEM((depth, 2 * vecs), BF16),
            pltpu.VMEM((sites, 128), F32),
            pltpu.VMEM((moms, 2, 2, 2, 32, vecs), F32),
            pltpu.VMEM((moms, 3, 2, 32, vecs), F32),
            pltpu.VMEM((moms, 2, 32, vecs), F32),
            pltpu.VMEM((moms, 2, 32, vecs), F32),
            pltpu.VMEM((pairs, 2, cols, 2 * vecs), F32),
            pltpu.VMEM((pairs, 2, cols, 2 * vecs), F32),
            pltpu.SemaphoreType.DMA((moms, 9)),
            pltpu.SemaphoreType.DMA((moms, 9)),
            pltpu.SemaphoreType.DMA((2, pairs)),
            pltpu.SemaphoreType.DMA((2, pairs)),
        ],
        compiler_params=pltpu.CompilerParams(
            collective_id=0, has_side_effects=True, vmem_limit_bytes=61 * 2**20
        ),
        name="correlators",
    )(momenta, eig_rows, per_rows, time_pairs)
    rows = pl.pallas_call(
        copy_kernel,
        out_shape=jax.ShapeDtypeStruct(rows.shape, F32),
        in_specs=[hbm],
        out_specs=hbm,
        scratch_shapes=[pltpu.SemaphoreType.DMA((PARTS,))],
        compiler_params=pltpu.CompilerParams(vmem_limit_bytes=62 * 2**20),
        name="result",
    )(rows)
    return (
        rows.reshape(cols, pairs, moms, 4, 2, vecs)
        .transpose(0, 1, 2, 4, 3, 5)
        .reshape(cols, pairs, moms, 2, order)
    )


PRECISE = lax.Precision.HIGHEST
SPIN_MIX = ((1.0, 0.0, 1.0, 0.0), (0.0, 1.0, 0.0, 1.0), (1.0, 0.0, 1.0, 0.0), (0.0, 1.0, 0.0, 1.0))
CHIRAL = (1.0, 1.0, -1.0, -1.0)


def spin_tables():
    spin_mix = jnp.array(SPIN_MIX, jnp.float32)
    chiral = jnp.array(CHIRAL, jnp.float32)
    spin_dressed = chiral[:, None] * spin_mix * chiral[None, :]
    return (spin_mix, spin_dressed)


def phase_tables(momenta, site_ids):
    coords = jnp.stack([site_ids % LS, site_ids // LS % LS, site_ids // (LS * LS)])
    phase_turns = jnp.mod(jnp.sum(momenta[:, :, None] * coords[None, :, :], axis=1), LS)
    phase_angle = phase_turns.astype(jnp.float32) * (2.0 * math.pi / LS)
    return (jnp.cos(phase_angle), jnp.sin(phase_angle))


def elemental_terms(vectors, cosine_tab, sine_tab):
    local_times = vectors.shape[0]
    vec_count = vectors.shape[4]
    real_part = vectors[:, :, :, 0, :]
    imag_part = vectors[:, :, :, 1, :]
    left_rows = vectors.reshape(local_times, -1, vec_count)
    per_moment = []
    for mom_index in range(cosine_tab.shape[0]):
        cos_here = cosine_tab[mom_index][None, None, :, None]
        sin_here = sine_tab[mom_index][None, None, :, None]
        turned_re = cos_here * real_part - sin_here * imag_part
        turned_im = sin_here * real_part + cos_here * imag_part
        first_half = jnp.stack([turned_re, turned_im], axis=3).reshape(local_times, -1, vec_count)
        second_half = jnp.stack([turned_im, -turned_re], axis=3).reshape(local_times, -1, vec_count)
        right_cols = jnp.concatenate([first_half, second_half], axis=2)
        product = jnp.einsum("tki,tkj->tij", left_rows, right_cols, precision=PRECISE)
        per_moment.append(
            product.reshape(local_times, vec_count, 2, vec_count).transpose(0, 2, 1, 3)
        )
    return jnp.stack(per_moment, axis=1)


def shards(eigvecs, perambulator, time_pairs, momenta):
    colour_count = eigvecs.shape[1]
    site_count = eigvecs.shape[2]
    vec_count = eigvecs.shape[4]
    slab_count = lax.axis_size("slab")
    site_ids = lax.axis_index("slab") * site_count + jnp.arange(site_count, dtype=jnp.int32)
    cosine_tab, sine_tab = phase_tables(momenta, site_ids)
    partial_sums = elemental_terms(eigvecs, cosine_tab, sine_tab)
    summed = lax.psum(partial_sums, "slab")
    all_times = lax.all_gather(summed, "tm", axis=0, tiled=True)
    all_times = all_times * (1.0 / math.sqrt(2.0 * colour_count * site_count * slab_count))
    sink_elem = jnp.take(all_times, time_pairs[:, 1], axis=0)
    source_elem = jnp.take(all_times, time_pairs[:, 0], axis=0)
    sink_re = sink_elem[:, :, 0]
    sink_im = sink_elem[:, :, 1]
    spin_mix, spin_dressed = spin_tables()
    panel_cols = perambulator.shape[0]
    pair_count = perambulator.shape[1]
    spin_order = perambulator.shape[3]
    spin_count = spin_order // vec_count
    mom_count = momenta.shape[0]
    panel_start = lax.axis_index("slab") * panel_cols
    panel_spin = panel_start // vec_count
    panel_vec = panel_start % vec_count
    chiral_col = lax.dynamic_index_in_dim(spin_dressed, panel_spin, 1, keepdims=False)
    source_block = lax.dynamic_slice_in_dim(source_elem, panel_vec, panel_cols, 3)
    dress_re = jnp.einsum("s,kmbi->kmsib", chiral_col, source_block[:, :, 0]).reshape(
        pair_count, mom_count, spin_order, panel_cols
    )
    dress_im = -jnp.einsum("s,kmbi->kmsib", chiral_col, source_block[:, :, 1]).reshape(
        pair_count, mom_count, spin_order, panel_cols
    )
    peram_piece = lax.all_gather(perambulator, "slab", axis=0, tiled=True)
    piece_re = peram_piece[:, :, 0]
    piece_im = peram_piece[:, :, 1]
    fold_re = jnp.einsum("ckr,kmcb->bkmr", piece_re, dress_re, precision=PRECISE) - jnp.einsum(
        "ckr,kmcb->bkmr", piece_im, dress_im, precision=PRECISE
    )
    fold_im = jnp.einsum("ckr,kmcb->bkmr", piece_re, dress_im, precision=PRECISE) + jnp.einsum(
        "ckr,kmcb->bkmr", piece_im, dress_re, precision=PRECISE
    )
    fold_re, fold_im = (fold_re, fold_im)
    fold_re = fold_re.reshape(panel_cols, pair_count, mom_count, spin_count, vec_count)
    fold_im = fold_im.reshape(panel_cols, pair_count, mom_count, spin_count, vec_count)
    mixed_re = jnp.einsum("bkmsj,kmij->bkmsi", fold_re, sink_re, precision=PRECISE) - jnp.einsum(
        "bkmsj,kmij->bkmsi", fold_im, sink_im, precision=PRECISE
    )
    mixed_im = jnp.einsum("bkmsj,kmij->bkmsi", fold_re, sink_im, precision=PRECISE) + jnp.einsum(
        "bkmsj,kmij->bkmsi", fold_im, sink_re, precision=PRECISE
    )
    final_re = jnp.einsum("ts,bkmsi->bkmti", spin_mix, mixed_re, precision=PRECISE).reshape(
        panel_cols, pair_count, mom_count, spin_order
    )
    final_im = jnp.einsum("ts,bkmsi->bkmti", spin_mix, mixed_im, precision=PRECISE).reshape(
        panel_cols, pair_count, mom_count, spin_order
    )
    dressed = jnp.stack([final_re, final_im], axis=3)
    return dressed


def solution(mesh):
    known = mesh.shape["tm"] == TIMES and mesh.shape["slab"] == SLABS
    return jax.shard_map(
        kernel_shards if known else shards,
        mesh=mesh,
        in_specs=(
            P("tm", None, "slab", None, None),
            P("slab", "tm", None, None),
            P("tm", None),
            P(),
        ),
        out_specs=P("slab", "tm", None, None, None),
        check_vma=False,
    )
```

```python
import functools
import math

import jax
import jax.numpy as jnp
from jax import lax
from jax.experimental import pallas as pl
from jax.experimental.pallas import tpu as pltpu
from jax.sharding import PartitionSpec as P

LS = 48
SLABS = 8
TIMES = 4
PARTS = 4
BF16 = jnp.bfloat16
F32 = jnp.float32
NN = (((1,), (0,)), ((), ()))
NT = (((1,), (1,)), ((), ()))


def split(value):
    high = value.astype(BF16)
    return high, (value - high.astype(F32)).astype(BF16)


def dot3(left, right, dims):
    def one(x, y):
        return lax.dot_general(x, y, dims, preferred_element_type=F32)

    return one(left[0], right[0]) + (one(left[0], right[1]) + one(left[1], right[0]))


def floor_div(value, by):
    return jnp.floor((value + 0.5) * (1.0 / by))


def correlator_kernel(
    scale, mom_hbm, eig_hbm, per_hbm, pairs_hbm, out_hbm,
    e_refs, d_ref, out_ref, out_sem, pairs_ref, mom_ref, eig_ref, per_ref, load_sem, left, rh, rl, phase, part, r1, h2, r3, psend, precv,
    send_sem, recv_sem, psend_sem, precv_sem,
):
    slab = lax.axis_index("slab")
    time = lax.axis_index("tm")
    core = slab % 2
    sub = (slab // 2) % 2
    sibling = slab + 1 - 2 * core
    near = slab + 2 - 4 * sub
    cross = near + 1 - 2 * core
    far = (slab + 4) % SLABS
    along_x = time + 1 - 2 * (time % 2)
    along_y = (time + 2) % TIMES
    first = along_x * (1 - core) + along_y * core
    second = along_y * (1 - core) + along_x * core
    tm_peers = (along_x, along_y)
    slab_peers = (sibling, near, cross, far)

    loads = [
        pltpu.make_async_copy(src, dst, load_sem.at[n])
        for n, (src, dst) in enumerate(
            ((per_hbm, per_ref), (mom_hbm, mom_ref), (eig_hbm, eig_ref), (pairs_hbm, pairs_ref))
        )
    ]
    for load in loads:
        load.start()

    barrier = pltpu.get_barrier_semaphore()
    for peer in slab_peers:
        pl.semaphore_signal(barrier, inc=1, device_id={"slab": peer}, device_id_type=pl.DeviceIdType.MESH)
    for peer in tm_peers:
        pl.semaphore_signal(barrier, inc=1, device_id={"tm": peer}, device_id_type=pl.DeviceIdType.MESH)

    loads[0].wait()
    pairs = psend.shape[0]
    cols = psend.shape[2]
    for k in range(pairs):
        for p in range(2):
            spins = [
                per_ref[pl.ds(k * 8 + t * 2 + p, cols, stride=8 * pairs), :] for t in range(4)
            ]
            psend[k, p, :, 0:128] = spins[0] + spins[2]
            psend[k, p, :, 128:256] = spins[1] + spins[3]

    pl.semaphore_wait(barrier, len(slab_peers) + len(tm_peers))

    def remote(src, dst, ssem, rsem, axis, peer):
        return pltpu.make_async_remote_copy(
            src_ref=src, dst_ref=dst, send_sem=ssem, recv_sem=rsem,
            device_id={axis: peer}, device_id_type=pl.DeviceIdType.MESH,
        )

    p_far = [
        remote(psend.at[k], precv.at[k], psend_sem.at[0, k], precv_sem.at[0, k], "slab", far)
        for k in range(pairs)
    ]
    p_core = [
        remote(d_ref.at[core, k], d_ref.at[core, k], psend_sem.at[1, k], precv_sem.at[1, k], "slab", sibling)
        for k in range(pairs)
    ]

    def difference(k):
        p_far[k].wait_recv()
        d_ref[core, k] = psend[k] - precv[k]
        p_core[k].start()

    p_far[0].start()
    loads[1].wait()

    moms = mom_ref.shape[0]
    sites = phase.shape[0]
    site = (lax.broadcasted_iota(jnp.int32, (sites, 128), 0) + slab * sites).astype(F32)
    lane = lax.broadcasted_iota(jnp.int32, (sites, 128), 1)
    row = floor_div(site, LS)
    plane = floor_div(row, LS)
    coords = (site - LS * row, row - LS * plane, plane)
    turns = jnp.zeros((sites, 128), F32)
    for m in range(moms):
        mine = mom_ref[m, 0].astype(F32) * coords[0]
        mine = mine + mom_ref[m, 1].astype(F32) * coords[1]
        mine = mine + mom_ref[m, 2].astype(F32) * coords[2]
        turns = jnp.where(lane % moms == m, mine, turns)
    turns = turns - LS * floor_div(turns, LS)
    turns = jnp.where(lane >= moms, turns - LS / 4, turns)
    phase[...] = jnp.cos(turns * (2.0 * math.pi / LS))

    loads[2].wait()
    wide = left.shape[1] // 2
    colours = eig_ref.shape[0] // (2 * sites)
    for c in range(colours):
        real = eig_ref[pl.ds(2 * sites * c, sites, stride=2), :]
        imag = eig_ref[pl.ds(2 * sites * c + 1, sites, stride=2), :]
        high, low = split(jnp.concatenate([real, imag], axis=1).T)
        left[c, :wide] = high
        left[c, wide:] = low

    sums = {}

    def compute(m, c):
        cosine = phase[:, m:m + 1]
        sine = phase[:, moms + m:moms + m + 1]
        real = eig_ref[pl.ds(2 * sites * c, sites, stride=2), :]
        imag = eig_ref[pl.ds(2 * sites * c + 1, sites, stride=2), :]
        turned = jnp.concatenate(
            [cosine * real - sine * imag, sine * real + cosine * imag], axis=1
        )
        high, low = split(turned)
        rh[...] = high
        rl[...] = low
        coarse = lax.dot_general(left[c], rh[...], NN, preferred_element_type=F32)
        fine = lax.dot_general(left[c, :wide], rl[...], NN, preferred_element_type=F32)
        got = coarse[:wide] + (coarse[wide:] + fine)
        sums[m] = got if c == 0 else sums[m] + got

    def spread(m):
        got = sums.pop(m)
        both = (
            got[:128, :128] + got[128:, 128:],
            got[:128, 128:] - got[128:, :128],
        )
        for half in range(2):
            for u in range(2):
                for p in range(2):
                    start = half * 64 + u * 32
                    part[m, half, u, p] = both[p][start:start + 32]

    steps = {}

    def step1(m):
        for n, (half, u, peer) in enumerate(
            ((1 - core, sub, sibling), (core, 1 - sub, near), (1 - core, 1 - sub, cross))
        ):
            steps[m, 1, n] = remote(
                part.at[m, half, u], r1.at[m, n], send_sem.at[m, n], recv_sem.at[m, n], "slab", peer
            )
            steps[m, 1, n].start()

    def step2(m):
        for n in range(3):
            steps[m, 1, n].wait_recv()
        h2[m] = (part[m, core, sub] + r1[m, 0]) + (r1[m, 1] + r1[m, 2])
        steps[m, 2] = remote(h2.at[m], r3.at[m], send_sem.at[m, 3], recv_sem.at[m, 3], "slab", far)
        steps[m, 2].start()

    def step3(m):
        steps[m, 2].wait_recv()
        e_refs[m][core, time, sub] = (h2[m] + r3[m]) * scale
        done = e_refs[m].at[core, time, sub]
        steps[m, 3] = remote(done, done, send_sem.at[m, 4], recv_sem.at[m, 4], "slab", near)
        steps[m, 3].start()

    def step4(m):
        steps[m, 3].wait_recv()
        done = e_refs[m].at[core, time]
        for n, peer in enumerate((first, second)):
            steps[m, 4, n] = remote(
                done, done, send_sem.at[m, 5 + n], recv_sem.at[m, 5 + n], "tm", peer
            )
            steps[m, 4, n].start()

    def step5(m):
        steps[m, 4, 0].wait_recv()
        done = e_refs[m].at[core, first]
        steps[m, 4, 2] = remote(done, done, send_sem.at[m, 7], recv_sem.at[m, 7], "tm", second)
        steps[m, 4, 2].start()

    def step6(m):
        steps[m, 4, 1].wait_recv()
        steps[m, 4, 2].wait_recv()
        done = e_refs[m].at[core]
        steps[m, 5] = remote(done, done, send_sem.at[m, 8], recv_sem.at[m, 8], "slab", sibling)
        steps[m, 5].start()

    def step7(m):
        steps[m, 5].wait_recv()
        if m == 0:
            p_core[0].wait_recv()
            loads[3].wait()
        dress(m, 0)

    rows_each = cols * 8

    def dress(m, k):
        e_ref = e_refs[m]
        t1 = pairs_ref[k, 0]
        t2 = pairs_ref[k, 1]

        def block(half, t, p):
            return e_ref[half, t, :, p].reshape(64, 128)

        source = split(jnp.concatenate([block(core, t1, 0), block(core, t1, 1)], axis=1))
        re_high, re_low = split(d_ref[:, k, 0].reshape(2 * cols, 256))
        im_high, im_low = split(d_ref[:, k, 1].reshape(2 * cols, 256))

        def wide_of(re, im):
            return jnp.concatenate(
                [jnp.concatenate([re, im], axis=1), jnp.concatenate([im, -re], axis=1)], axis=0
            )

        fold = dot3(source, (wide_of(re_high, im_high), wide_of(re_low, im_low)), NN)
        spun = jnp.concatenate(
            [
                jnp.concatenate([fold[:, 0:128], fold[:, 256:384]], axis=1),
                jnp.concatenate([fold[:, 128:256], fold[:, 384:512]], axis=1),
            ],
            axis=0,
        )
        sink = [
            split(jnp.concatenate([block(0, t2, p), block(1, t2, p)], axis=0)) for p in range(2)
        ]

        def tall_of(re, im):
            return jnp.concatenate(
                [jnp.concatenate([re, -im], axis=1), jnp.concatenate([im, re], axis=1)], axis=0
            )

        right = tuple(tall_of(sink[0][n], sink[1][n]) for n in range(2))
        got = dot3(split(spun), right, NT)
        for t in range(4):
            for p in range(2):
                start = (m * pairs + k) * rows_each + t * 2 + p
                out_ref[pl.ds(start, cols, stride=8), :] = got[
                    64 * (t % 2):64 * (t % 2 + 1), 128 * p:128 * (p + 1)
                ]
        stores[m, k] = pltpu.make_async_copy(
            out_ref.at[pl.ds((m * pairs + k) * rows_each, rows_each)].reshape(cols, 8, 128),
            out_hbm.at[:, k, m],
            out_sem.at[m, k],
        )
        stores[m, k].start()

    stores = {}
    stages = (step1, step2, step3, step4, step5, step6, step7)
    offsets = (0, 1, 3, 4, 6, 7, 9)
    plan = {}
    for m in range(moms):
        ready = colours * (m + 1) - 1
        for stage, offset in zip(stages, offsets):
            plan.setdefault(ready + offset, []).append((stage, m))
    last = max(plan)
    for tick in range(last):
        if tick < colours * moms:
            compute(tick // colours, tick % colours)
            if tick % colours == colours - 1:
                spread(tick // colours)
        for stage, m in plan.get(tick, ()):
            stage(m)
        if tick == colours * (moms - 1):
            difference(0)
        if tick == colours * (moms - 1) - 1:
            for k in range(1, pairs):
                p_far[k].start()
        if tick == last - 2:
            for k in range(1, pairs):
                difference(k)
    for k in range(1, pairs):
        p_core[k].wait_recv()
        for m in range(moms - 1):
            dress(m, k)
    step7(moms - 1)
    for k in range(1, pairs):
        dress(moms - 1, k)

    for copy in p_far + p_core:
        copy.wait_send()
    for copy in steps.values():
        copy.wait_send()
    for store in stores.values():
        store.wait()


def copy_kernel(src, dst, held, in_sem, out_sem):
    share = src.shape[0] // PARTS
    loads, stores = [], []
    for n in range(PARTS):
        part = pl.ds(n * share, share)
        loads.append(pltpu.make_async_copy(src.at[part], held.at[part], in_sem.at[n]))
        stores.append(pltpu.make_async_copy(held.at[part], dst.at[part], out_sem.at[n]))
    for load in loads:
        load.start()
    for load, store in zip(loads, stores):
        load.wait()
        store.start()
    for store in stores:
        store.wait()


def kernel_shards(eigvecs, perambulator, time_pairs, momenta):
    _, colours, sites, _, vecs = eigvecs.shape
    cols, pairs, _, order = perambulator.shape
    moms = momenta.shape[0]
    scale = 1.0 / math.sqrt(2.0 * colours * sites * SLABS)
    eig_rows = eigvecs.reshape(colours * sites * 2, vecs)
    per_rows = (
        perambulator.reshape(cols, pairs, 2, 4, vecs)
        .transpose(0, 1, 3, 2, 4)
        .reshape(cols * pairs * 8, vecs)
    )
    hbm = pl.BlockSpec(memory_space=pltpu.HBM)
    rows = pl.pallas_call(
        functools.partial(correlator_kernel, scale),
        out_shape=jax.ShapeDtypeStruct((cols, pairs, moms, 8, vecs), F32),
        in_specs=[hbm, hbm, hbm, hbm],
        out_specs=hbm,
        scratch_shapes=[
            [pltpu.VMEM((2, TIMES, 2, 2, 32, vecs), F32) for _ in range(moms)],
            pltpu.VMEM((2, pairs, 2, cols, 2 * vecs), F32),
            pltpu.VMEM((moms * cols * pairs * 8, vecs), F32),
            pltpu.SemaphoreType.DMA((moms, pairs)),
            pltpu.SMEM(time_pairs.shape, jnp.int32),
            pltpu.SMEM(momenta.shape, jnp.int32),
            pltpu.VMEM(eig_rows.shape, F32),
            pltpu.VMEM(per_rows.shape, F32),
            pltpu.SemaphoreType.DMA((4,)),
            pltpu.VMEM((colours, 4 * vecs, sites), BF16),
            pltpu.VMEM((sites, 2 * vecs), BF16),
            pltpu.VMEM((sites, 2 * vecs), BF16),
            pltpu.VMEM((sites, 128), F32),
            pltpu.VMEM((moms, 2, 2, 2, 32, vecs), F32),
            pltpu.VMEM((moms, 3, 2, 32, vecs), F32),
            pltpu.VMEM((moms, 2, 32, vecs), F32),
            pltpu.VMEM((moms, 2, 32, vecs), F32),
            pltpu.VMEM((pairs, 2, cols, 2 * vecs), F32),
            pltpu.VMEM((pairs, 2, cols, 2 * vecs), F32),
            pltpu.SemaphoreType.DMA((moms, 9)),
            pltpu.SemaphoreType.DMA((moms, 9)),
            pltpu.SemaphoreType.DMA((2, pairs)),
            pltpu.SemaphoreType.DMA((2, pairs)),
        ],
        compiler_params=pltpu.CompilerParams(
            collective_id=0, has_side_effects=True, vmem_limit_bytes=61 * 2**20
        ),
        name="correlators",
    )(momenta, eig_rows, per_rows, time_pairs)
    rows = pl.pallas_call(
        copy_kernel,
        out_shape=jax.ShapeDtypeStruct(rows.shape, F32),
        in_specs=[hbm],
        out_specs=hbm,
        scratch_shapes=[
            pltpu.VMEM(rows.shape, F32),
            pltpu.SemaphoreType.DMA((PARTS,)),
            pltpu.SemaphoreType.DMA((PARTS,)),
        ],
        compiler_params=pltpu.CompilerParams(vmem_limit_bytes=62 * 2**20),
        name="result",
    )(rows)
    return (
        rows.reshape(cols, pairs, moms, 4, 2, vecs)
        .transpose(0, 1, 2, 4, 3, 5)
        .reshape(cols, pairs, moms, 2, order)
    )


PRECISE = lax.Precision.HIGHEST
SPIN_MIX = ((1.0, 0.0, 1.0, 0.0), (0.0, 1.0, 0.0, 1.0), (1.0, 0.0, 1.0, 0.0), (0.0, 1.0, 0.0, 1.0))
CHIRAL = (1.0, 1.0, -1.0, -1.0)


def spin_tables():
    spin_mix = jnp.array(SPIN_MIX, jnp.float32)
    chiral = jnp.array(CHIRAL, jnp.float32)
    spin_dressed = chiral[:, None] * spin_mix * chiral[None, :]
    return (spin_mix, spin_dressed)


def phase_tables(momenta, site_ids):
    coords = jnp.stack([site_ids % LS, site_ids // LS % LS, site_ids // (LS * LS)])
    phase_turns = jnp.mod(jnp.sum(momenta[:, :, None] * coords[None, :, :], axis=1), LS)
    phase_angle = phase_turns.astype(jnp.float32) * (2.0 * math.pi / LS)
    return (jnp.cos(phase_angle), jnp.sin(phase_angle))


def elemental_terms(vectors, cosine_tab, sine_tab):
    local_times = vectors.shape[0]
    vec_count = vectors.shape[4]
    real_part = vectors[:, :, :, 0, :]
    imag_part = vectors[:, :, :, 1, :]
    left_rows = vectors.reshape(local_times, -1, vec_count)
    per_moment = []
    for mom_index in range(cosine_tab.shape[0]):
        cos_here = cosine_tab[mom_index][None, None, :, None]
        sin_here = sine_tab[mom_index][None, None, :, None]
        turned_re = cos_here * real_part - sin_here * imag_part
        turned_im = sin_here * real_part + cos_here * imag_part
        first_half = jnp.stack([turned_re, turned_im], axis=3).reshape(local_times, -1, vec_count)
        second_half = jnp.stack([turned_im, -turned_re], axis=3).reshape(local_times, -1, vec_count)
        right_cols = jnp.concatenate([first_half, second_half], axis=2)
        product = jnp.einsum("tki,tkj->tij", left_rows, right_cols, precision=PRECISE)
        per_moment.append(
            product.reshape(local_times, vec_count, 2, vec_count).transpose(0, 2, 1, 3)
        )
    return jnp.stack(per_moment, axis=1)


def shards(eigvecs, perambulator, time_pairs, momenta):
    colour_count = eigvecs.shape[1]
    site_count = eigvecs.shape[2]
    vec_count = eigvecs.shape[4]
    slab_count = lax.axis_size("slab")
    site_ids = lax.axis_index("slab") * site_count + jnp.arange(site_count, dtype=jnp.int32)
    cosine_tab, sine_tab = phase_tables(momenta, site_ids)
    partial_sums = elemental_terms(eigvecs, cosine_tab, sine_tab)
    summed = lax.psum(partial_sums, "slab")
    all_times = lax.all_gather(summed, "tm", axis=0, tiled=True)
    all_times = all_times * (1.0 / math.sqrt(2.0 * colour_count * site_count * slab_count))
    sink_elem = jnp.take(all_times, time_pairs[:, 1], axis=0)
    source_elem = jnp.take(all_times, time_pairs[:, 0], axis=0)
    sink_re = sink_elem[:, :, 0]
    sink_im = sink_elem[:, :, 1]
    spin_mix, spin_dressed = spin_tables()
    panel_cols = perambulator.shape[0]
    pair_count = perambulator.shape[1]
    spin_order = perambulator.shape[3]
    spin_count = spin_order // vec_count
    mom_count = momenta.shape[0]
    panel_start = lax.axis_index("slab") * panel_cols
    panel_spin = panel_start // vec_count
    panel_vec = panel_start % vec_count
    chiral_col = lax.dynamic_index_in_dim(spin_dressed, panel_spin, 1, keepdims=False)
    source_block = lax.dynamic_slice_in_dim(source_elem, panel_vec, panel_cols, 3)
    dress_re = jnp.einsum("s,kmbi->kmsib", chiral_col, source_block[:, :, 0]).reshape(
        pair_count, mom_count, spin_order, panel_cols
    )
    dress_im = -jnp.einsum("s,kmbi->kmsib", chiral_col, source_block[:, :, 1]).reshape(
        pair_count, mom_count, spin_order, panel_cols
    )
    peram_piece = lax.all_gather(perambulator, "slab", axis=0, tiled=True)
    piece_re = peram_piece[:, :, 0]
    piece_im = peram_piece[:, :, 1]
    fold_re = jnp.einsum("ckr,kmcb->bkmr", piece_re, dress_re, precision=PRECISE) - jnp.einsum(
        "ckr,kmcb->bkmr", piece_im, dress_im, precision=PRECISE
    )
    fold_im = jnp.einsum("ckr,kmcb->bkmr", piece_re, dress_im, precision=PRECISE) + jnp.einsum(
        "ckr,kmcb->bkmr", piece_im, dress_re, precision=PRECISE
    )
    fold_re, fold_im = (fold_re, fold_im)
    fold_re = fold_re.reshape(panel_cols, pair_count, mom_count, spin_count, vec_count)
    fold_im = fold_im.reshape(panel_cols, pair_count, mom_count, spin_count, vec_count)
    mixed_re = jnp.einsum("bkmsj,kmij->bkmsi", fold_re, sink_re, precision=PRECISE) - jnp.einsum(
        "bkmsj,kmij->bkmsi", fold_im, sink_im, precision=PRECISE
    )
    mixed_im = jnp.einsum("bkmsj,kmij->bkmsi", fold_re, sink_im, precision=PRECISE) + jnp.einsum(
        "bkmsj,kmij->bkmsi", fold_im, sink_re, precision=PRECISE
    )
    final_re = jnp.einsum("ts,bkmsi->bkmti", spin_mix, mixed_re, precision=PRECISE).reshape(
        panel_cols, pair_count, mom_count, spin_order
    )
    final_im = jnp.einsum("ts,bkmsi->bkmti", spin_mix, mixed_im, precision=PRECISE).reshape(
        panel_cols, pair_count, mom_count, spin_order
    )
    dressed = jnp.stack([final_re, final_im], axis=3)
    return dressed


def solution(mesh):
    known = mesh.shape["tm"] == TIMES and mesh.shape["slab"] == SLABS
    return jax.shard_map(
        kernel_shards if known else shards,
        mesh=mesh,
        in_specs=(
            P("tm", None, "slab", None, None),
            P("slab", "tm", None, None),
            P("tm", None),
            P(),
        ),
        out_specs=P("slab", "tm", None, None, None),
        check_vma=False,
    )
```

```python
import functools
import math

import jax
import jax.numpy as jnp
from jax import lax
from jax.experimental import pallas as pl
from jax.experimental.pallas import tpu as pltpu
from jax.sharding import PartitionSpec as P

LS = 48
SLABS = 8
TIMES = 4
PARTS = 4
BF16 = jnp.bfloat16
F32 = jnp.float32
NN = (((1,), (0,)), ((), ()))
NT = (((1,), (1,)), ((), ()))


def split(value):
    high = value.astype(BF16)
    return high, (value - high.astype(F32)).astype(BF16)


def dot3(left, right, dims):
    def one(x, y):
        return lax.dot_general(x, y, dims, preferred_element_type=F32)

    return one(left[0], right[0]) + (one(left[0], right[1]) + one(left[1], right[0]))


def floor_div(value, by):
    return jnp.floor((value + 0.5) * (1.0 / by))


def correlator_kernel(
    scale, mom_hbm, eig_hbm, per_hbm, pairs_hbm, out_hbm,
    e_refs, d_ref, out_ref, out_sem, pairs_ref, mom_ref, eig_ref, per_ref, load_sem, left, rh, rl, phase, part, r1, h2, r3, psend, precv,
    send_sem, recv_sem, psend_sem, precv_sem,
):
    slab = lax.axis_index("slab")
    time = lax.axis_index("tm")
    core = slab % 2
    sub = (slab // 2) % 2
    sibling = slab + 1 - 2 * core
    near = slab + 2 - 4 * sub
    cross = near + 1 - 2 * core
    far = (slab + 4) % SLABS
    along_x = time + 1 - 2 * (time % 2)
    along_y = (time + 2) % TIMES
    first = along_x * (1 - core) + along_y * core
    second = along_y * (1 - core) + along_x * core
    tm_peers = (along_x, along_y)
    slab_peers = (sibling, near, cross, far)

    loads = [
        pltpu.make_async_copy(src, dst, load_sem.at[n])
        for n, (src, dst) in enumerate(
            ((per_hbm, per_ref), (mom_hbm, mom_ref), (eig_hbm, eig_ref), (pairs_hbm, pairs_ref))
        )
    ]
    for load in loads:
        load.start()

    barrier = pltpu.get_barrier_semaphore()
    for peer in slab_peers:
        pl.semaphore_signal(barrier, inc=1, device_id={"slab": peer}, device_id_type=pl.DeviceIdType.MESH)
    for peer in tm_peers:
        pl.semaphore_signal(barrier, inc=1, device_id={"tm": peer}, device_id_type=pl.DeviceIdType.MESH)

    loads[0].wait()
    pairs = psend.shape[0]
    cols = psend.shape[2]
    for k in range(pairs):
        for p in range(2):
            spins = [
                per_ref[pl.ds(k * 8 + t * 2 + p, cols, stride=8 * pairs), :] for t in range(4)
            ]
            psend[k, p, :, 0:128] = spins[0] + spins[2]
            psend[k, p, :, 128:256] = spins[1] + spins[3]

    pl.semaphore_wait(barrier, len(slab_peers) + len(tm_peers))

    def remote(src, dst, ssem, rsem, axis, peer):
        return pltpu.make_async_remote_copy(
            src_ref=src, dst_ref=dst, send_sem=ssem, recv_sem=rsem,
            device_id={axis: peer}, device_id_type=pl.DeviceIdType.MESH,
        )

    p_far = [
        remote(psend.at[k], precv.at[k], psend_sem.at[0, k], precv_sem.at[0, k], "slab", far)
        for k in range(pairs)
    ]
    p_core = [
        remote(d_ref.at[core, k], d_ref.at[core, k], psend_sem.at[1, k], precv_sem.at[1, k], "slab", sibling)
        for k in range(pairs)
    ]

    def difference(k):
        p_far[k].wait_recv()
        d_ref[core, k] = psend[k] - precv[k]
        p_core[k].start()

    p_far[0].start()
    loads[1].wait()

    moms = mom_ref.shape[0]
    sites = phase.shape[0]
    site = (lax.broadcasted_iota(jnp.int32, (sites, 128), 0) + slab * sites).astype(F32)
    lane = lax.broadcasted_iota(jnp.int32, (sites, 128), 1)
    row = floor_div(site, LS)
    plane = floor_div(row, LS)
    coords = (site - LS * row, row - LS * plane, plane)
    turns = jnp.zeros((sites, 128), F32)
    for m in range(moms):
        mine = mom_ref[m, 0].astype(F32) * coords[0]
        mine = mine + mom_ref[m, 1].astype(F32) * coords[1]
        mine = mine + mom_ref[m, 2].astype(F32) * coords[2]
        turns = jnp.where(lane % moms == m, mine, turns)
    turns = turns - LS * floor_div(turns, LS)
    turns = jnp.where(lane >= moms, turns - LS / 4, turns)
    phase[...] = jnp.cos(turns * (2.0 * math.pi / LS))

    loads[2].wait()
    rows = []
    wide = left.shape[0] // 2
    colours = eig_ref.shape[0] // (2 * sites)
    for c in range(colours):
        real = eig_ref[pl.ds(2 * sites * c, sites, stride=2), :]
        imag = eig_ref[pl.ds(2 * sites * c + 1, sites, stride=2), :]
        rows.append(jnp.concatenate([real, imag], axis=1))
    high, low = split(jnp.concatenate(rows, axis=0).T)
    left[:wide] = high
    left[wide:] = low

    def compute(m):
        cosine = phase[:, m:m + 1]
        sine = phase[:, moms + m:moms + m + 1]
        for c in range(colours):
            real = eig_ref[pl.ds(2 * sites * c, sites, stride=2), :]
            imag = eig_ref[pl.ds(2 * sites * c + 1, sites, stride=2), :]
            turned = jnp.concatenate(
                [cosine * real - sine * imag, sine * real + cosine * imag], axis=1
            )
            high, low = split(turned)
            rh[c * sites:(c + 1) * sites, :] = high
            rl[c * sites:(c + 1) * sites, :] = low
        coarse = lax.dot_general(left[...], rh[...], NN, preferred_element_type=F32)
        fine = lax.dot_general(left[:wide], rl[...], NN, preferred_element_type=F32)
        got = coarse[:wide] + (coarse[wide:] + fine)
        both = (
            got[:128, :128] + got[128:, 128:],
            got[:128, 128:] - got[128:, :128],
        )
        for half in range(2):
            for u in range(2):
                for p in range(2):
                    start = half * 64 + u * 32
                    part[m, half, u, p] = both[p][start:start + 32]

    steps = {}

    def step1(m):
        for n, (half, u, peer) in enumerate(
            ((1 - core, sub, sibling), (core, 1 - sub, near), (1 - core, 1 - sub, cross))
        ):
            steps[m, 1, n] = remote(
                part.at[m, half, u], r1.at[m, n], send_sem.at[m, n], recv_sem.at[m, n], "slab", peer
            )
            steps[m, 1, n].start()

    def step2(m):
        for n in range(3):
            steps[m, 1, n].wait_recv()
        h2[m] = (part[m, core, sub] + r1[m, 0]) + (r1[m, 1] + r1[m, 2])
        steps[m, 2] = remote(h2.at[m], r3.at[m], send_sem.at[m, 3], recv_sem.at[m, 3], "slab", far)
        steps[m, 2].start()

    def step3(m):
        steps[m, 2].wait_recv()
        e_refs[m][core, time, sub] = (h2[m] + r3[m]) * scale
        done = e_refs[m].at[core, time, sub]
        steps[m, 3] = remote(done, done, send_sem.at[m, 4], recv_sem.at[m, 4], "slab", near)
        steps[m, 3].start()

    def step4(m):
        steps[m, 3].wait_recv()
        done = e_refs[m].at[core, time]
        for n, peer in enumerate((first, second)):
            steps[m, 4, n] = remote(
                done, done, send_sem.at[m, 5 + n], recv_sem.at[m, 5 + n], "tm", peer
            )
            steps[m, 4, n].start()

    def step5(m):
        steps[m, 4, 0].wait_recv()
        done = e_refs[m].at[core, first]
        steps[m, 4, 2] = remote(done, done, send_sem.at[m, 7], recv_sem.at[m, 7], "tm", second)
        steps[m, 4, 2].start()

    def step6(m):
        steps[m, 4, 1].wait_recv()
        steps[m, 4, 2].wait_recv()
        done = e_refs[m].at[core]
        steps[m, 5] = remote(done, done, send_sem.at[m, 8], recv_sem.at[m, 8], "slab", sibling)
        steps[m, 5].start()

    def step7(m):
        steps[m, 5].wait_recv()

    rows_each = cols * 8

    def dress(m, k):
        e_ref = e_refs[m]
        t1 = pairs_ref[k, 0]
        t2 = pairs_ref[k, 1]

        def block(half, t, p):
            return e_ref[half, t, :, p].reshape(64, 128)

        source = split(jnp.concatenate([block(core, t1, 0), block(core, t1, 1)], axis=1))
        re_high, re_low = split(d_ref[:, k, 0].reshape(2 * cols, 256))
        im_high, im_low = split(d_ref[:, k, 1].reshape(2 * cols, 256))

        def wide_of(re, im):
            return jnp.concatenate(
                [jnp.concatenate([re, im], axis=1), jnp.concatenate([im, -re], axis=1)], axis=0
            )

        fold = dot3(source, (wide_of(re_high, im_high), wide_of(re_low, im_low)), NN)
        spun = jnp.concatenate(
            [
                jnp.concatenate([fold[:, 0:128], fold[:, 256:384]], axis=1),
                jnp.concatenate([fold[:, 128:256], fold[:, 384:512]], axis=1),
            ],
            axis=0,
        )
        sink = [
            split(jnp.concatenate([block(0, t2, p), block(1, t2, p)], axis=0)) for p in range(2)
        ]

        def tall_of(re, im):
            return jnp.concatenate(
                [jnp.concatenate([re, -im], axis=1), jnp.concatenate([im, re], axis=1)], axis=0
            )

        right = tuple(tall_of(sink[0][n], sink[1][n]) for n in range(2))
        got = dot3(split(spun), right, NT)
        for t in range(4):
            for p in range(2):
                start = (m * pairs + k) * rows_each + t * 2 + p
                out_ref[pl.ds(start, cols, stride=8), :] = got[
                    64 * (t % 2):64 * (t % 2 + 1), 128 * p:128 * (p + 1)
                ]
        stores[m, k] = pltpu.make_async_copy(
            out_ref.at[pl.ds((m * pairs + k) * rows_each, rows_each)].reshape(cols, 8, 128),
            out_hbm.at[:, k, m],
            out_sem.at[m, k],
        )
        stores[m, k].start()

    stores = {}
    stages = (step1, step2, step3, step4, step5, step6, step7)
    loads[3].wait()
    ticks = moms + len(stages) - 1
    for tick in range(ticks - 1):
        if tick < moms:
            compute(tick)
        if tick == moms - 2:
            for k in range(1, pairs):
                p_far[k].start()
        arrived = None
        for m in range(moms):
            if 0 <= tick - m < len(stages):
                stages[tick - m](m)
                if stages[tick - m] is step7:
                    arrived = m
        if tick == moms + 1:
            difference(0)
        if tick == ticks - 2:
            for k in range(1, pairs):
                difference(k)
        if arrived is not None:
            if arrived == 0:
                p_core[0].wait_recv()
            dress(arrived, 0)
    for k in range(1, pairs):
        p_core[k].wait_recv()
        for m in range(moms - 1):
            dress(m, k)
    step7(moms - 1)
    for k in range(pairs):
        dress(moms - 1, k)

    for copy in p_far + p_core:
        copy.wait_send()
    for copy in steps.values():
        copy.wait_send()
    for store in stores.values():
        store.wait()


def copy_kernel(src, dst, held, in_sem, out_sem):
    share = src.shape[0] // PARTS
    loads, stores = [], []
    for n in range(PARTS):
        part = pl.ds(n * share, share)
        loads.append(pltpu.make_async_copy(src.at[part], held.at[part], in_sem.at[n]))
        stores.append(pltpu.make_async_copy(held.at[part], dst.at[part], out_sem.at[n]))
    for load in loads:
        load.start()
    for load, store in zip(loads, stores):
        load.wait()
        store.start()
    for store in stores:
        store.wait()


def kernel_shards(eigvecs, perambulator, time_pairs, momenta):
    _, colours, sites, _, vecs = eigvecs.shape
    cols, pairs, _, order = perambulator.shape
    moms = momenta.shape[0]
    scale = 1.0 / math.sqrt(2.0 * colours * sites * SLABS)
    eig_rows = eigvecs.reshape(colours * sites * 2, vecs)
    per_rows = (
        perambulator.reshape(cols, pairs, 2, 4, vecs)
        .transpose(0, 1, 3, 2, 4)
        .reshape(cols * pairs * 8, vecs)
    )
    depth = colours * sites
    hbm = pl.BlockSpec(memory_space=pltpu.HBM)
    rows = pl.pallas_call(
        functools.partial(correlator_kernel, scale),
        out_shape=jax.ShapeDtypeStruct((cols, pairs, moms, 8, vecs), F32),
        in_specs=[hbm, hbm, hbm, hbm],
        out_specs=hbm,
        scratch_shapes=[
            [pltpu.VMEM((2, TIMES, 2, 2, 32, vecs), F32) for _ in range(moms)],
            pltpu.VMEM((2, pairs, 2, cols, 2 * vecs), F32),
            pltpu.VMEM((moms * cols * pairs * 8, vecs), F32),
            pltpu.SemaphoreType.DMA((moms, pairs)),
            pltpu.SMEM(time_pairs.shape, jnp.int32),
            pltpu.SMEM(momenta.shape, jnp.int32),
            pltpu.VMEM(eig_rows.shape, F32),
            pltpu.VMEM(per_rows.shape, F32),
            pltpu.SemaphoreType.DMA((4,)),
            pltpu.VMEM((4 * vecs, depth), BF16),
            pltpu.VMEM((depth, 2 * vecs), BF16),
            pltpu.VMEM((depth, 2 * vecs), BF16),
            pltpu.VMEM((sites, 128), F32),
            pltpu.VMEM((moms, 2, 2, 2, 32, vecs), F32),
            pltpu.VMEM((moms, 3, 2, 32, vecs), F32),
            pltpu.VMEM((moms, 2, 32, vecs), F32),
            pltpu.VMEM((moms, 2, 32, vecs), F32),
            pltpu.VMEM((pairs, 2, cols, 2 * vecs), F32),
            pltpu.VMEM((pairs, 2, cols, 2 * vecs), F32),
            pltpu.SemaphoreType.DMA((moms, 9)),
            pltpu.SemaphoreType.DMA((moms, 9)),
            pltpu.SemaphoreType.DMA((2, pairs)),
            pltpu.SemaphoreType.DMA((2, pairs)),
        ],
        compiler_params=pltpu.CompilerParams(
            collective_id=0, has_side_effects=True, vmem_limit_bytes=61 * 2**20
        ),
        name="correlators",
    )(momenta, eig_rows, per_rows, time_pairs)
    rows = pl.pallas_call(
        copy_kernel,
        out_shape=jax.ShapeDtypeStruct(rows.shape, F32),
        in_specs=[hbm],
        out_specs=hbm,
        scratch_shapes=[
            pltpu.VMEM(rows.shape, F32),
            pltpu.SemaphoreType.DMA((PARTS,)),
            pltpu.SemaphoreType.DMA((PARTS,)),
        ],
        compiler_params=pltpu.CompilerParams(vmem_limit_bytes=62 * 2**20),
        name="result",
    )(rows)
    return (
        rows.reshape(cols, pairs, moms, 4, 2, vecs)
        .transpose(0, 1, 2, 4, 3, 5)
        .reshape(cols, pairs, moms, 2, order)
    )


PRECISE = lax.Precision.HIGHEST
SPIN_MIX = ((1.0, 0.0, 1.0, 0.0), (0.0, 1.0, 0.0, 1.0), (1.0, 0.0, 1.0, 0.0), (0.0, 1.0, 0.0, 1.0))
CHIRAL = (1.0, 1.0, -1.0, -1.0)


def spin_tables():
    spin_mix = jnp.array(SPIN_MIX, jnp.float32)
    chiral = jnp.array(CHIRAL, jnp.float32)
    spin_dressed = chiral[:, None] * spin_mix * chiral[None, :]
    return (spin_mix, spin_dressed)


def phase_tables(momenta, site_ids):
    coords = jnp.stack([site_ids % LS, site_ids // LS % LS, site_ids // (LS * LS)])
    phase_turns = jnp.mod(jnp.sum(momenta[:, :, None] * coords[None, :, :], axis=1), LS)
    phase_angle = phase_turns.astype(jnp.float32) * (2.0 * math.pi / LS)
    return (jnp.cos(phase_angle), jnp.sin(phase_angle))


def elemental_terms(vectors, cosine_tab, sine_tab):
    local_times = vectors.shape[0]
    vec_count = vectors.shape[4]
    real_part = vectors[:, :, :, 0, :]
    imag_part = vectors[:, :, :, 1, :]
    left_rows = vectors.reshape(local_times, -1, vec_count)
    per_moment = []
    for mom_index in range(cosine_tab.shape[0]):
        cos_here = cosine_tab[mom_index][None, None, :, None]
        sin_here = sine_tab[mom_index][None, None, :, None]
        turned_re = cos_here * real_part - sin_here * imag_part
        turned_im = sin_here * real_part + cos_here * imag_part
        first_half = jnp.stack([turned_re, turned_im], axis=3).reshape(local_times, -1, vec_count)
        second_half = jnp.stack([turned_im, -turned_re], axis=3).reshape(local_times, -1, vec_count)
        right_cols = jnp.concatenate([first_half, second_half], axis=2)
        product = jnp.einsum("tki,tkj->tij", left_rows, right_cols, precision=PRECISE)
        per_moment.append(
            product.reshape(local_times, vec_count, 2, vec_count).transpose(0, 2, 1, 3)
        )
    return jnp.stack(per_moment, axis=1)


def shards(eigvecs, perambulator, time_pairs, momenta):
    colour_count = eigvecs.shape[1]
    site_count = eigvecs.shape[2]
    vec_count = eigvecs.shape[4]
    slab_count = lax.axis_size("slab")
    site_ids = lax.axis_index("slab") * site_count + jnp.arange(site_count, dtype=jnp.int32)
    cosine_tab, sine_tab = phase_tables(momenta, site_ids)
    partial_sums = elemental_terms(eigvecs, cosine_tab, sine_tab)
    summed = lax.psum(partial_sums, "slab")
    all_times = lax.all_gather(summed, "tm", axis=0, tiled=True)
    all_times = all_times * (1.0 / math.sqrt(2.0 * colour_count * site_count * slab_count))
    sink_elem = jnp.take(all_times, time_pairs[:, 1], axis=0)
    source_elem = jnp.take(all_times, time_pairs[:, 0], axis=0)
    sink_re = sink_elem[:, :, 0]
    sink_im = sink_elem[:, :, 1]
    spin_mix, spin_dressed = spin_tables()
    panel_cols = perambulator.shape[0]
    pair_count = perambulator.shape[1]
    spin_order = perambulator.shape[3]
    spin_count = spin_order // vec_count
    mom_count = momenta.shape[0]
    panel_start = lax.axis_index("slab") * panel_cols
    panel_spin = panel_start // vec_count
    panel_vec = panel_start % vec_count
    chiral_col = lax.dynamic_index_in_dim(spin_dressed, panel_spin, 1, keepdims=False)
    source_block = lax.dynamic_slice_in_dim(source_elem, panel_vec, panel_cols, 3)
    dress_re = jnp.einsum("s,kmbi->kmsib", chiral_col, source_block[:, :, 0]).reshape(
        pair_count, mom_count, spin_order, panel_cols
    )
    dress_im = -jnp.einsum("s,kmbi->kmsib", chiral_col, source_block[:, :, 1]).reshape(
        pair_count, mom_count, spin_order, panel_cols
    )
    peram_piece = lax.all_gather(perambulator, "slab", axis=0, tiled=True)
    piece_re = peram_piece[:, :, 0]
    piece_im = peram_piece[:, :, 1]
    fold_re = jnp.einsum("ckr,kmcb->bkmr", piece_re, dress_re, precision=PRECISE) - jnp.einsum(
        "ckr,kmcb->bkmr", piece_im, dress_im, precision=PRECISE
    )
    fold_im = jnp.einsum("ckr,kmcb->bkmr", piece_re, dress_im, precision=PRECISE) + jnp.einsum(
        "ckr,kmcb->bkmr", piece_im, dress_re, precision=PRECISE
    )
    fold_re, fold_im = (fold_re, fold_im)
    fold_re = fold_re.reshape(panel_cols, pair_count, mom_count, spin_count, vec_count)
    fold_im = fold_im.reshape(panel_cols, pair_count, mom_count, spin_count, vec_count)
    mixed_re = jnp.einsum("bkmsj,kmij->bkmsi", fold_re, sink_re, precision=PRECISE) - jnp.einsum(
        "bkmsj,kmij->bkmsi", fold_im, sink_im, precision=PRECISE
    )
    mixed_im = jnp.einsum("bkmsj,kmij->bkmsi", fold_re, sink_im, precision=PRECISE) + jnp.einsum(
        "bkmsj,kmij->bkmsi", fold_im, sink_re, precision=PRECISE
    )
    final_re = jnp.einsum("ts,bkmsi->bkmti", spin_mix, mixed_re, precision=PRECISE).reshape(
        panel_cols, pair_count, mom_count, spin_order
    )
    final_im = jnp.einsum("ts,bkmsi->bkmti", spin_mix, mixed_im, precision=PRECISE).reshape(
        panel_cols, pair_count, mom_count, spin_order
    )
    dressed = jnp.stack([final_re, final_im], axis=3)
    return dressed


def solution(mesh):
    known = mesh.shape["tm"] == TIMES and mesh.shape["slab"] == SLABS
    return jax.shard_map(
        kernel_shards if known else shards,
        mesh=mesh,
        in_specs=(
            P("tm", None, "slab", None, None),
            P("slab", "tm", None, None),
            P("tm", None),
            P(),
        ),
        out_specs=P("slab", "tm", None, None, None),
        check_vma=False,
    )
```

```python
import functools
import math

import jax
import jax.numpy as jnp
from jax import lax
from jax.experimental import pallas as pl
from jax.experimental.pallas import tpu as pltpu
from jax.sharding import PartitionSpec as P

LS = 48
SLABS = 8
TIMES = 4
PARTS = 4
BF16 = jnp.bfloat16
F32 = jnp.float32
NN = (((1,), (0,)), ((), ()))
NT = (((1,), (1,)), ((), ()))


def split(value):
    high = value.astype(BF16)
    return high, (value - high.astype(F32)).astype(BF16)


def dot3(left, right, dims):
    def one(x, y):
        return lax.dot_general(x, y, dims, preferred_element_type=F32)

    return one(left[0], right[0]) + (one(left[0], right[1]) + one(left[1], right[0]))


def floor_div(value, by):
    return jnp.floor((value + 0.5) * (1.0 / by))


def correlator_kernel(
    scale, sites, mom_hbm, eig_hbm, per_hbm, pairs_hbm, out_hbm,
    e_refs, d_ref, out_ref, out_sem, pairs_ref, mom_ref, eig_ref, per_ref, load_sem, left, rh, rl, flat, phase, part, r1, h2, r3, psend, precv,
    send_sem, recv_sem, psend_sem, precv_sem,
):
    slab = lax.axis_index("slab")
    time = lax.axis_index("tm")
    core = slab % 2
    sub = (slab // 2) % 2
    sibling = slab + 1 - 2 * core
    near = slab + 2 - 4 * sub
    cross = near + 1 - 2 * core
    far = (slab + 4) % SLABS
    tm_peers = (time + 1 - 2 * (time % 2), (time + 2) % TIMES, TIMES - 1 - time)
    slab_peers = (sibling, near, cross, far)

    loads = [
        pltpu.make_async_copy(src, dst, load_sem.at[n])
        for n, (src, dst) in enumerate(
            ((per_hbm, per_ref), (mom_hbm, mom_ref), (eig_hbm, eig_ref), (pairs_hbm, pairs_ref))
        )
    ]
    for load in loads:
        load.start()

    barrier = pltpu.get_barrier_semaphore()
    for peer in slab_peers:
        pl.semaphore_signal(barrier, inc=1, device_id={"slab": peer}, device_id_type=pl.DeviceIdType.MESH)
    for peer in tm_peers:
        pl.semaphore_signal(barrier, inc=1, device_id={"tm": peer}, device_id_type=pl.DeviceIdType.MESH)

    loads[0].wait()
    pairs = psend.shape[0]
    cols = psend.shape[2]
    for k in range(pairs):
        for p in range(2):
            spins = [
                per_ref[pl.ds(k * 8 + t * 2 + p, cols, stride=8 * pairs), :] for t in range(4)
            ]
            psend[k, p, :, 0:128] = spins[0] + spins[2]
            psend[k, p, :, 128:256] = spins[1] + spins[3]

    pl.semaphore_wait(barrier, len(slab_peers) + len(tm_peers))

    def remote(src, dst, ssem, rsem, axis, peer):
        return pltpu.make_async_remote_copy(
            src_ref=src, dst_ref=dst, send_sem=ssem, recv_sem=rsem,
            device_id={axis: peer}, device_id_type=pl.DeviceIdType.MESH,
        )

    p_far = [
        remote(psend.at[k], precv.at[k], psend_sem.at[0, k], precv_sem.at[0, k], "slab", far)
        for k in range(pairs)
    ]
    p_core = [
        remote(d_ref.at[core, k], d_ref.at[core, k], psend_sem.at[1, k], precv_sem.at[1, k], "slab", sibling)
        for k in range(pairs)
    ]

    def difference(k):
        p_far[k].wait_recv()
        d_ref[core, k] = psend[k] - precv[k]
        p_core[k].start()

    p_far[0].start()
    loads[1].wait()

    moms = mom_ref.shape[0]
    colours = eig_ref.shape[0] // (2 * sites)
    depth = colours * sites
    place = lax.broadcasted_iota(jnp.int32, (2 * moms, depth), 1).astype(F32)
    kind = lax.broadcasted_iota(jnp.int32, (2 * moms, depth), 0)
    site = place - sites * floor_div(place, sites) + (slab * sites).astype(F32)
    row = floor_div(site, LS)
    plane = floor_div(row, LS)
    coords = (site - LS * row, row - LS * plane, plane)
    turns = jnp.zeros((2 * moms, depth), F32)
    for m in range(moms):
        mine = mom_ref[m, 0].astype(F32) * coords[0]
        mine = mine + mom_ref[m, 1].astype(F32) * coords[1]
        mine = mine + mom_ref[m, 2].astype(F32) * coords[2]
        turns = jnp.where(kind % moms == m, mine, turns)
    turns = turns - LS * floor_div(turns, LS)
    turns = jnp.where(kind >= moms, turns - LS / 4, turns)
    phase[...] = jnp.cos(turns * (2.0 * math.pi / LS))

    loads[2].wait()
    vecs = eig_ref.shape[1]
    wide = 2 * vecs
    rows = []
    for c in range(colours):
        real = eig_ref[pl.ds(2 * sites * c, sites, stride=2), :]
        imag = eig_ref[pl.ds(2 * sites * c + 1, sites, stride=2), :]
        rows.append(jnp.concatenate([real, imag], axis=1))
    whole = jnp.concatenate(rows, axis=0)
    high, low = split(whole)
    rh[...] = high
    rl[...] = low
    flat[...] = whole.T

    def turn(m):
        cosine = phase[m:m + 1, :]
        sine = phase[moms + m:moms + m + 1, :]
        real = flat[:vecs, :]
        imag = flat[vecs:, :]
        slot = m % 2
        for n, value in enumerate(
            (cosine * real - sine * imag, sine * real + cosine * imag)
        ):
            high, low = split(value)
            left[slot, n * vecs:(n + 1) * vecs] = high
            left[slot, wide + n * vecs:wide + (n + 1) * vecs] = low

    def compute(m):
        slot = m % 2
        coarse = lax.dot_general(left[slot], rh[...], NN, preferred_element_type=F32)
        fine = lax.dot_general(left[slot, :wide], rl[...], NN, preferred_element_type=F32)
        if m + 1 < moms:
            turn(m + 1)
        got = coarse[:wide] + (coarse[wide:] + fine)
        both = (
            (got[:vecs, :vecs] + got[vecs:, vecs:]).T,
            (got[vecs:, :vecs] - got[:vecs, vecs:]).T,
        )
        for half in range(2):
            for u in range(2):
                for p in range(2):
                    start = half * 64 + u * 32
                    part[m, half, u, p] = both[p][start:start + 32]

    steps = {}

    def step1(m):
        for n, (half, u, peer) in enumerate(
            ((1 - core, sub, sibling), (core, 1 - sub, near), (1 - core, 1 - sub, cross))
        ):
            steps[m, 1, n] = remote(
                part.at[m, half, u], r1.at[m, n], send_sem.at[m, n], recv_sem.at[m, n], "slab", peer
            )
            steps[m, 1, n].start()

    def step2(m):
        for n in range(3):
            steps[m, 1, n].wait_recv()
        h2[m] = (part[m, core, sub] + r1[m, 0]) + (r1[m, 1] + r1[m, 2])
        steps[m, 2] = remote(h2.at[m], r3.at[m], send_sem.at[m, 3], recv_sem.at[m, 3], "slab", far)
        steps[m, 2].start()

    def step3(m):
        steps[m, 2].wait_recv()
        e_refs[m][core, time, sub] = (h2[m] + r3[m]) * scale
        done = e_refs[m].at[core, time, sub]
        steps[m, 3] = remote(done, done, send_sem.at[m, 4], recv_sem.at[m, 4], "slab", near)
        steps[m, 3].start()

    def step4(m):
        steps[m, 3].wait_recv()
        done = e_refs[m].at[core, time]
        for n, peer in enumerate(tm_peers):
            steps[m, 4, n] = remote(
                done, done, send_sem.at[m, 5 + n], recv_sem.at[m, 5 + n], "tm", peer
            )
            steps[m, 4, n].start()

    def step5(m):
        for n in range(len(tm_peers)):
            steps[m, 4, n].wait_recv()
        done = e_refs[m].at[core]
        steps[m, 5] = remote(done, done, send_sem.at[m, 8], recv_sem.at[m, 8], "slab", sibling)
        steps[m, 5].start()

    def step6(m):
        steps[m, 5].wait_recv()

    rows_each = cols * 8

    def dress(m, k):
        e_ref = e_refs[m]
        t1 = pairs_ref[k, 0]
        t2 = pairs_ref[k, 1]

        def block(half, t, p):
            return e_ref[half, t, :, p].reshape(64, 128)

        source = split(jnp.concatenate([block(core, t1, 0), block(core, t1, 1)], axis=1))
        re_high, re_low = split(d_ref[:, k, 0].reshape(2 * cols, 256))
        im_high, im_low = split(d_ref[:, k, 1].reshape(2 * cols, 256))

        def wide_of(re, im):
            return jnp.concatenate(
                [jnp.concatenate([re, im], axis=1), jnp.concatenate([im, -re], axis=1)], axis=0
            )

        fold = dot3(source, (wide_of(re_high, im_high), wide_of(re_low, im_low)), NN)
        spun = jnp.concatenate(
            [
                jnp.concatenate([fold[:, 0:128], fold[:, 256:384]], axis=1),
                jnp.concatenate([fold[:, 128:256], fold[:, 384:512]], axis=1),
            ],
            axis=0,
        )
        sink = [
            split(jnp.concatenate([block(0, t2, p), block(1, t2, p)], axis=0)) for p in range(2)
        ]

        def tall_of(re, im):
            return jnp.concatenate(
                [jnp.concatenate([re, -im], axis=1), jnp.concatenate([im, re], axis=1)], axis=0
            )

        right = tuple(tall_of(sink[0][n], sink[1][n]) for n in range(2))
        got = dot3(split(spun), right, NT)
        for t in range(4):
            for p in range(2):
                start = (m * pairs + k) * rows_each + t * 2 + p
                out_ref[pl.ds(start, cols, stride=8), :] = got[
                    64 * (t % 2):64 * (t % 2 + 1), 128 * p:128 * (p + 1)
                ]
        stores[m, k] = pltpu.make_async_copy(
            out_ref.at[pl.ds((m * pairs + k) * rows_each, rows_each)].reshape(cols, 8, 128),
            out_hbm.at[:, k, m],
            out_sem.at[m, k],
        )
        stores[m, k].start()

    stores = {}
    stages = (step1, step2, step3, step4, step5, step6)
    loads[3].wait()
    turn(0)
    ticks = moms + len(stages) - 1
    for tick in range(ticks - 1):
        if tick < moms:
            compute(tick)
        arrived = None
        for m in range(moms):
            if 0 <= tick - m < len(stages):
                stages[tick - m](m)
                if stages[tick - m] is step6:
                    arrived = m
        if tick == moms - 1:
            for k in range(1, pairs):
                p_far[k].start()
        if tick == moms:
            difference(0)
        if tick == ticks - 2:
            for k in range(1, pairs):
                difference(k)
        if arrived is not None:
            if arrived == 0:
                p_core[0].wait_recv()
            dress(arrived, 0)
    for k in range(1, pairs):
        p_core[k].wait_recv()
        for m in range(moms - 1):
            dress(m, k)
    step6(moms - 1)
    for k in range(pairs):
        dress(moms - 1, k)

    for copy in p_far + p_core:
        copy.wait_send()
    for copy in steps.values():
        copy.wait_send()
    for store in stores.values():
        store.wait()


def copy_kernel(src, dst, held, in_sem, out_sem):
    share = src.shape[0] // PARTS
    loads, stores = [], []
    for n in range(PARTS):
        part = pl.ds(n * share, share)
        loads.append(pltpu.make_async_copy(src.at[part], held.at[part], in_sem.at[n]))
        stores.append(pltpu.make_async_copy(held.at[part], dst.at[part], out_sem.at[n]))
    for load in loads:
        load.start()
    for load, store in zip(loads, stores):
        load.wait()
        store.start()
    for store in stores:
        store.wait()


def kernel_shards(eigvecs, perambulator, time_pairs, momenta):
    _, colours, sites, _, vecs = eigvecs.shape
    cols, pairs, _, order = perambulator.shape
    moms = momenta.shape[0]
    scale = 1.0 / math.sqrt(2.0 * colours * sites * SLABS)
    eig_rows = eigvecs.reshape(colours * sites * 2, vecs)
    per_rows = (
        perambulator.reshape(cols, pairs, 2, 4, vecs)
        .transpose(0, 1, 3, 2, 4)
        .reshape(cols * pairs * 8, vecs)
    )
    depth = colours * sites
    hbm = pl.BlockSpec(memory_space=pltpu.HBM)
    rows = pl.pallas_call(
        functools.partial(correlator_kernel, scale, sites),
        out_shape=jax.ShapeDtypeStruct((cols, pairs, moms, 8, vecs), F32),
        in_specs=[hbm, hbm, hbm, hbm],
        out_specs=hbm,
        scratch_shapes=[
            [pltpu.VMEM((2, TIMES, 2, 2, 32, vecs), F32) for _ in range(moms)],
            pltpu.VMEM((2, pairs, 2, cols, 2 * vecs), F32),
            pltpu.VMEM((moms * cols * pairs * 8, vecs), F32),
            pltpu.SemaphoreType.DMA((moms, pairs)),
            pltpu.SMEM(time_pairs.shape, jnp.int32),
            pltpu.SMEM(momenta.shape, jnp.int32),
            pltpu.VMEM(eig_rows.shape, F32),
            pltpu.VMEM(per_rows.shape, F32),
            pltpu.SemaphoreType.DMA((4,)),
            pltpu.VMEM((2, 4 * vecs, depth), BF16),
            pltpu.VMEM((depth, 2 * vecs), BF16),
            pltpu.VMEM((depth, 2 * vecs), BF16),
            pltpu.VMEM((2 * vecs, depth), F32),
            pltpu.VMEM((2 * moms, depth), F32),
            pltpu.VMEM((moms, 2, 2, 2, 32, vecs), F32),
            pltpu.VMEM((moms, 3, 2, 32, vecs), F32),
            pltpu.VMEM((moms, 2, 32, vecs), F32),
            pltpu.VMEM((moms, 2, 32, vecs), F32),
            pltpu.VMEM((pairs, 2, cols, 2 * vecs), F32),
            pltpu.VMEM((pairs, 2, cols, 2 * vecs), F32),
            pltpu.SemaphoreType.DMA((moms, 9)),
            pltpu.SemaphoreType.DMA((moms, 9)),
            pltpu.SemaphoreType.DMA((2, pairs)),
            pltpu.SemaphoreType.DMA((2, pairs)),
        ],
        compiler_params=pltpu.CompilerParams(
            collective_id=0, has_side_effects=True, vmem_limit_bytes=61 * 2**20
        ),
        name="correlators",
    )(momenta, eig_rows, per_rows, time_pairs)
    rows = pl.pallas_call(
        copy_kernel,
        out_shape=jax.ShapeDtypeStruct(rows.shape, F32),
        in_specs=[hbm],
        out_specs=hbm,
        scratch_shapes=[
            pltpu.VMEM(rows.shape, F32),
            pltpu.SemaphoreType.DMA((PARTS,)),
            pltpu.SemaphoreType.DMA((PARTS,)),
        ],
        compiler_params=pltpu.CompilerParams(vmem_limit_bytes=62 * 2**20),
        name="result",
    )(rows)
    return (
        rows.reshape(cols, pairs, moms, 4, 2, vecs)
        .transpose(0, 1, 2, 4, 3, 5)
        .reshape(cols, pairs, moms, 2, order)
    )


PRECISE = lax.Precision.HIGHEST
SPIN_MIX = ((1.0, 0.0, 1.0, 0.0), (0.0, 1.0, 0.0, 1.0), (1.0, 0.0, 1.0, 0.0), (0.0, 1.0, 0.0, 1.0))
CHIRAL = (1.0, 1.0, -1.0, -1.0)


def spin_tables():
    spin_mix = jnp.array(SPIN_MIX, jnp.float32)
    chiral = jnp.array(CHIRAL, jnp.float32)
    spin_dressed = chiral[:, None] * spin_mix * chiral[None, :]
    return (spin_mix, spin_dressed)


def phase_tables(momenta, site_ids):
    coords = jnp.stack([site_ids % LS, site_ids // LS % LS, site_ids // (LS * LS)])
    phase_turns = jnp.mod(jnp.sum(momenta[:, :, None] * coords[None, :, :], axis=1), LS)
    phase_angle = phase_turns.astype(jnp.float32) * (2.0 * math.pi / LS)
    return (jnp.cos(phase_angle), jnp.sin(phase_angle))


def elemental_terms(vectors, cosine_tab, sine_tab):
    local_times = vectors.shape[0]
    vec_count = vectors.shape[4]
    real_part = vectors[:, :, :, 0, :]
    imag_part = vectors[:, :, :, 1, :]
    left_rows = vectors.reshape(local_times, -1, vec_count)
    per_moment = []
    for mom_index in range(cosine_tab.shape[0]):
        cos_here = cosine_tab[mom_index][None, None, :, None]
        sin_here = sine_tab[mom_index][None, None, :, None]
        turned_re = cos_here * real_part - sin_here * imag_part
        turned_im = sin_here * real_part + cos_here * imag_part
        first_half = jnp.stack([turned_re, turned_im], axis=3).reshape(local_times, -1, vec_count)
        second_half = jnp.stack([turned_im, -turned_re], axis=3).reshape(local_times, -1, vec_count)
        right_cols = jnp.concatenate([first_half, second_half], axis=2)
        product = jnp.einsum("tki,tkj->tij", left_rows, right_cols, precision=PRECISE)
        per_moment.append(
            product.reshape(local_times, vec_count, 2, vec_count).transpose(0, 2, 1, 3)
        )
    return jnp.stack(per_moment, axis=1)


def shards(eigvecs, perambulator, time_pairs, momenta):
    colour_count = eigvecs.shape[1]
    site_count = eigvecs.shape[2]
    vec_count = eigvecs.shape[4]
    slab_count = lax.axis_size("slab")
    site_ids = lax.axis_index("slab") * site_count + jnp.arange(site_count, dtype=jnp.int32)
    cosine_tab, sine_tab = phase_tables(momenta, site_ids)
    partial_sums = elemental_terms(eigvecs, cosine_tab, sine_tab)
    summed = lax.psum(partial_sums, "slab")
    all_times = lax.all_gather(summed, "tm", axis=0, tiled=True)
    all_times = all_times * (1.0 / math.sqrt(2.0 * colour_count * site_count * slab_count))
    sink_elem = jnp.take(all_times, time_pairs[:, 1], axis=0)
    source_elem = jnp.take(all_times, time_pairs[:, 0], axis=0)
    sink_re = sink_elem[:, :, 0]
    sink_im = sink_elem[:, :, 1]
    spin_mix, spin_dressed = spin_tables()
    panel_cols = perambulator.shape[0]
    pair_count = perambulator.shape[1]
    spin_order = perambulator.shape[3]
    spin_count = spin_order // vec_count
    mom_count = momenta.shape[0]
    panel_start = lax.axis_index("slab") * panel_cols
    panel_spin = panel_start // vec_count
    panel_vec = panel_start % vec_count
    chiral_col = lax.dynamic_index_in_dim(spin_dressed, panel_spin, 1, keepdims=False)
    source_block = lax.dynamic_slice_in_dim(source_elem, panel_vec, panel_cols, 3)
    dress_re = jnp.einsum("s,kmbi->kmsib", chiral_col, source_block[:, :, 0]).reshape(
        pair_count, mom_count, spin_order, panel_cols
    )
    dress_im = -jnp.einsum("s,kmbi->kmsib", chiral_col, source_block[:, :, 1]).reshape(
        pair_count, mom_count, spin_order, panel_cols
    )
    peram_piece = lax.all_gather(perambulator, "slab", axis=0, tiled=True)
    piece_re = peram_piece[:, :, 0]
    piece_im = peram_piece[:, :, 1]
    fold_re = jnp.einsum("ckr,kmcb->bkmr", piece_re, dress_re, precision=PRECISE) - jnp.einsum(
        "ckr,kmcb->bkmr", piece_im, dress_im, precision=PRECISE
    )
    fold_im = jnp.einsum("ckr,kmcb->bkmr", piece_re, dress_im, precision=PRECISE) + jnp.einsum(
        "ckr,kmcb->bkmr", piece_im, dress_re, precision=PRECISE
    )
    fold_re, fold_im = (fold_re, fold_im)
    fold_re = fold_re.reshape(panel_cols, pair_count, mom_count, spin_count, vec_count)
    fold_im = fold_im.reshape(panel_cols, pair_count, mom_count, spin_count, vec_count)
    mixed_re = jnp.einsum("bkmsj,kmij->bkmsi", fold_re, sink_re, precision=PRECISE) - jnp.einsum(
        "bkmsj,kmij->bkmsi", fold_im, sink_im, precision=PRECISE
    )
    mixed_im = jnp.einsum("bkmsj,kmij->bkmsi", fold_re, sink_im, precision=PRECISE) + jnp.einsum(
        "bkmsj,kmij->bkmsi", fold_im, sink_re, precision=PRECISE
    )
    final_re = jnp.einsum("ts,bkmsi->bkmti", spin_mix, mixed_re, precision=PRECISE).reshape(
        panel_cols, pair_count, mom_count, spin_order
    )
    final_im = jnp.einsum("ts,bkmsi->bkmti", spin_mix, mixed_im, precision=PRECISE).reshape(
        panel_cols, pair_count, mom_count, spin_order
    )
    dressed = jnp.stack([final_re, final_im], axis=3)
    return dressed


def solution(mesh):
    known = mesh.shape["tm"] == TIMES and mesh.shape["slab"] == SLABS
    return jax.shard_map(
        kernel_shards if known else shards,
        mesh=mesh,
        in_specs=(
            P("tm", None, "slab", None, None),
            P("slab", "tm", None, None),
            P("tm", None),
            P(),
        ),
        out_specs=P("slab", "tm", None, None, None),
        check_vma=False,
    )
```

```python
import functools
import math

import jax
import jax.numpy as jnp
from jax import lax
from jax.experimental import pallas as pl
from jax.experimental.pallas import tpu as pltpu
from jax.sharding import PartitionSpec as P

LS = 48
SLABS = 8
TIMES = 4
PARTS = 4
BF16 = jnp.bfloat16
F32 = jnp.float32
NN = (((1,), (0,)), ((), ()))
NT = (((1,), (1,)), ((), ()))


def split(value):
    high = value.astype(BF16)
    return high, (value - high.astype(F32)).astype(BF16)


def dot3(left, right, dims):
    def one(x, y):
        return lax.dot_general(x, y, dims, preferred_element_type=F32)

    return one(left[0], right[0]) + (one(left[0], right[1]) + one(left[1], right[0]))


def floor_div(value, by):
    return jnp.floor((value + 0.5) * (1.0 / by))


def correlator_kernel(
    scale, sites, mom_hbm, eig_hbm, per_hbm, pairs_hbm, out_hbm,
    e_refs, d_ref, out_ref, out_sem, pairs_ref, mom_ref, eig_ref, per_ref, load_sem, left, rh, rl, flat, phase, part, r1, h2, r3, psend, precv,
    send_sem, recv_sem, psend_sem, precv_sem,
):
    slab = lax.axis_index("slab")
    time = lax.axis_index("tm")
    core = slab % 2
    sub = (slab // 2) % 2
    sibling = slab + 1 - 2 * core
    near = slab + 2 - 4 * sub
    cross = near + 1 - 2 * core
    far = (slab + 4) % SLABS
    tm_peers = (time + 1 - 2 * (time % 2), (time + 2) % TIMES, TIMES - 1 - time)
    slab_peers = (sibling, near, cross, far)

    loads = [
        pltpu.make_async_copy(src, dst, load_sem.at[n])
        for n, (src, dst) in enumerate(
            ((per_hbm, per_ref), (mom_hbm, mom_ref), (eig_hbm, eig_ref), (pairs_hbm, pairs_ref))
        )
    ]
    for load in loads:
        load.start()

    barrier = pltpu.get_barrier_semaphore()
    for peer in slab_peers:
        pl.semaphore_signal(barrier, inc=1, device_id={"slab": peer}, device_id_type=pl.DeviceIdType.MESH)
    for peer in tm_peers:
        pl.semaphore_signal(barrier, inc=1, device_id={"tm": peer}, device_id_type=pl.DeviceIdType.MESH)

    loads[0].wait()
    pairs = psend.shape[0]
    cols = psend.shape[2]
    for k in range(pairs):
        for p in range(2):
            spins = [
                per_ref[pl.ds(k * 8 + t * 2 + p, cols, stride=8 * pairs), :] for t in range(4)
            ]
            psend[k, p, :, 0:128] = spins[0] + spins[2]
            psend[k, p, :, 128:256] = spins[1] + spins[3]

    pl.semaphore_wait(barrier, len(slab_peers) + len(tm_peers))

    def remote(src, dst, ssem, rsem, axis, peer):
        return pltpu.make_async_remote_copy(
            src_ref=src, dst_ref=dst, send_sem=ssem, recv_sem=rsem,
            device_id={axis: peer}, device_id_type=pl.DeviceIdType.MESH,
        )

    pieces = [(p, pl.ds(16 * j, 16)) for p in range(2) for j in range(cols // 16)]

    def start(copies):
        for copy in copies:
            copy.start()

    def wait_recv(copies):
        for copy in copies:
            copy.wait_recv()

    p_far = [
        [
            remote(
                psend.at[k, p, part_rows], precv.at[k, p, part_rows],
                psend_sem.at[0, k, n], precv_sem.at[0, k, n], "slab", far,
            )
            for n, (p, part_rows) in enumerate(pieces)
        ]
        for k in range(pairs)
    ]
    p_core = [
        [
            remote(
                d_ref.at[core, k, p], d_ref.at[core, k, p],
                psend_sem.at[1, k, p], precv_sem.at[1, k, p], "slab", sibling,
            )
            for p in range(2)
        ]
        for k in range(pairs)
    ]

    def difference(k):
        wait_recv(p_far[k])
        d_ref[core, k] = psend[k] - precv[k]
        start(p_core[k])

    start(p_far[0])
    loads[1].wait()

    moms = mom_ref.shape[0]
    colours = eig_ref.shape[0] // (2 * sites)
    depth = colours * sites
    place = lax.broadcasted_iota(jnp.int32, (2 * moms, depth), 1).astype(F32)
    kind = lax.broadcasted_iota(jnp.int32, (2 * moms, depth), 0)
    site = place - sites * floor_div(place, sites) + (slab * sites).astype(F32)
    row = floor_div(site, LS)
    plane = floor_div(row, LS)
    coords = (site - LS * row, row - LS * plane, plane)
    turns = jnp.zeros((2 * moms, depth), F32)
    for m in range(moms):
        mine = mom_ref[m, 0].astype(F32) * coords[0]
        mine = mine + mom_ref[m, 1].astype(F32) * coords[1]
        mine = mine + mom_ref[m, 2].astype(F32) * coords[2]
        turns = jnp.where(kind % moms == m, mine, turns)
    turns = turns - LS * floor_div(turns, LS)
    turns = jnp.where(kind >= moms, turns - LS / 4, turns)
    phase[...] = jnp.cos(turns * (2.0 * math.pi / LS))

    loads[2].wait()
    vecs = eig_ref.shape[1]
    wide = 2 * vecs
    rows = []
    for c in range(colours):
        real = eig_ref[pl.ds(2 * sites * c, sites, stride=2), :]
        imag = eig_ref[pl.ds(2 * sites * c + 1, sites, stride=2), :]
        rows.append(jnp.concatenate([real, imag], axis=1))
    whole = jnp.concatenate(rows, axis=0)
    high, low = split(whole)
    rh[...] = high
    rl[...] = low
    flat[...] = whole.T

    def turn(m):
        cosine = phase[m:m + 1, :]
        sine = phase[moms + m:moms + m + 1, :]
        real = flat[:vecs, :]
        imag = flat[vecs:, :]
        slot = m % 2
        for n, value in enumerate(
            (cosine * real - sine * imag, sine * real + cosine * imag)
        ):
            high, low = split(value)
            left[slot, n * vecs:(n + 1) * vecs] = high
            left[slot, wide + n * vecs:wide + (n + 1) * vecs] = low

    def compute(m):
        slot = m % 2
        coarse = lax.dot_general(left[slot], rh[...], NN, preferred_element_type=F32)
        fine = lax.dot_general(left[slot, :wide], rl[...], NN, preferred_element_type=F32)
        if m + 1 < moms:
            turn(m + 1)
        got = coarse[:wide] + (coarse[wide:] + fine)
        both = (
            (got[:vecs, :vecs] + got[vecs:, vecs:]).T,
            (got[vecs:, :vecs] - got[:vecs, vecs:]).T,
        )
        for half in range(2):
            for u in range(2):
                for p in range(2):
                    start = half * 64 + u * 32
                    part[m, half, u, p] = both[p][start:start + 32]

    steps = {}

    def step1(m):
        for n, (half, u, peer) in enumerate(
            ((1 - core, sub, sibling), (core, 1 - sub, near), (1 - core, 1 - sub, cross))
        ):
            steps[m, 1, n] = remote(
                part.at[m, half, u], r1.at[m, n], send_sem.at[m, n], recv_sem.at[m, n], "slab", peer
            )
            steps[m, 1, n].start()

    def step2(m):
        for n in range(3):
            steps[m, 1, n].wait_recv()
        h2[m] = (part[m, core, sub] + r1[m, 0]) + (r1[m, 1] + r1[m, 2])
        steps[m, 2] = remote(h2.at[m], r3.at[m], send_sem.at[m, 3], recv_sem.at[m, 3], "slab", far)
        steps[m, 2].start()

    def step3(m):
        steps[m, 2].wait_recv()
        e_refs[m][core, time, sub] = (h2[m] + r3[m]) * scale
        done = e_refs[m].at[core, time, sub]
        steps[m, 3] = remote(done, done, send_sem.at[m, 4], recv_sem.at[m, 4], "slab", near)
        steps[m, 3].start()

    def step4(m):
        steps[m, 3].wait_recv()
        for u in range(2):
            done = e_refs[m].at[core, time, u]
            for n, peer in enumerate(tm_peers):
                spot = 5 + 3 * u + n
                steps[m, 4, u, n] = remote(
                    done, done, send_sem.at[m, spot], recv_sem.at[m, spot], "tm", peer
                )
                steps[m, 4, u, n].start()

    def step5(m):
        for u in range(2):
            for n in range(len(tm_peers)):
                steps[m, 4, u, n].wait_recv()
        for t in range(TIMES):
            done = e_refs[m].at[core, t]
            steps[m, 5, t] = remote(
                done, done, send_sem.at[m, 11 + t], recv_sem.at[m, 11 + t], "slab", sibling
            )
            steps[m, 5, t].start()

    def step6(m):
        for t in range(TIMES):
            steps[m, 5, t].wait_recv()

    rows_each = cols * 8

    def dress(m, k):
        e_ref = e_refs[m]
        t1 = pairs_ref[k, 0]
        t2 = pairs_ref[k, 1]

        def block(half, t, p):
            return e_ref[half, t, :, p].reshape(64, 128)

        source = split(jnp.concatenate([block(core, t1, 0), block(core, t1, 1)], axis=1))
        re_high, re_low = split(d_ref[:, k, 0].reshape(2 * cols, 256))
        im_high, im_low = split(d_ref[:, k, 1].reshape(2 * cols, 256))

        def wide_of(re, im):
            return jnp.concatenate(
                [jnp.concatenate([re, im], axis=1), jnp.concatenate([im, -re], axis=1)], axis=0
            )

        fold = dot3(source, (wide_of(re_high, im_high), wide_of(re_low, im_low)), NN)
        spun = jnp.concatenate(
            [
                jnp.concatenate([fold[:, 0:128], fold[:, 256:384]], axis=1),
                jnp.concatenate([fold[:, 128:256], fold[:, 384:512]], axis=1),
            ],
            axis=0,
        )
        sink = [
            split(jnp.concatenate([block(0, t2, p), block(1, t2, p)], axis=0)) for p in range(2)
        ]

        def tall_of(re, im):
            return jnp.concatenate(
                [jnp.concatenate([re, -im], axis=1), jnp.concatenate([im, re], axis=1)], axis=0
            )

        right = tuple(tall_of(sink[0][n], sink[1][n]) for n in range(2))
        got = dot3(split(spun), right, NT)
        for t in range(4):
            for p in range(2):
                start = (m * pairs + k) * rows_each + t * 2 + p
                out_ref[pl.ds(start, cols, stride=8), :] = got[
                    64 * (t % 2):64 * (t % 2 + 1), 128 * p:128 * (p + 1)
                ]
        stores[m, k] = pltpu.make_async_copy(
            out_ref.at[pl.ds((m * pairs + k) * rows_each, rows_each)].reshape(cols, 8, 128),
            out_hbm.at[:, k, m],
            out_sem.at[m, k],
        )
        stores[m, k].start()

    stores = {}
    stages = (step1, step2, step3, step4, step5, step6)
    loads[3].wait()
    turn(0)
    ticks = moms + len(stages) - 1
    for tick in range(ticks - 1):
        if tick < moms:
            compute(tick)
        arrived = None
        for m in range(moms):
            if 0 <= tick - m < len(stages):
                stages[tick - m](m)
                if stages[tick - m] is step6:
                    arrived = m
        if tick == moms - 1:
            for k in range(1, pairs):
                start(p_far[k])
        if tick == moms:
            difference(0)
        if tick == ticks - 2:
            for k in range(1, pairs):
                difference(k)
        if arrived is not None:
            if arrived == 0:
                wait_recv(p_core[0])
            dress(arrived, 0)
    for k in range(1, pairs):
        wait_recv(p_core[k])
        for m in range(moms - 1):
            dress(m, k)
    step6(moms - 1)
    for k in range(pairs):
        dress(moms - 1, k)

    for copies in p_far + p_core:
        for copy in copies:
            copy.wait_send()
    for copy in steps.values():
        copy.wait_send()
    for store in stores.values():
        store.wait()


def copy_kernel(src, dst, held, in_sem, out_sem):
    share = src.shape[0] // PARTS
    loads, stores = [], []
    for n in range(PARTS):
        part = pl.ds(n * share, share)
        loads.append(pltpu.make_async_copy(src.at[part], held.at[part], in_sem.at[n]))
        stores.append(pltpu.make_async_copy(held.at[part], dst.at[part], out_sem.at[n]))
    for load in loads:
        load.start()
    for load, store in zip(loads, stores):
        load.wait()
        store.start()
    for store in stores:
        store.wait()


def kernel_shards(eigvecs, perambulator, time_pairs, momenta):
    _, colours, sites, _, vecs = eigvecs.shape
    cols, pairs, _, order = perambulator.shape
    moms = momenta.shape[0]
    scale = 1.0 / math.sqrt(2.0 * colours * sites * SLABS)
    eig_rows = eigvecs.reshape(colours * sites * 2, vecs)
    per_rows = (
        perambulator.reshape(cols, pairs, 2, 4, vecs)
        .transpose(0, 1, 3, 2, 4)
        .reshape(cols * pairs * 8, vecs)
    )
    depth = colours * sites
    hbm = pl.BlockSpec(memory_space=pltpu.HBM)
    rows = pl.pallas_call(
        functools.partial(correlator_kernel, scale, sites),
        out_shape=jax.ShapeDtypeStruct((cols, pairs, moms, 8, vecs), F32),
        in_specs=[hbm, hbm, hbm, hbm],
        out_specs=hbm,
        scratch_shapes=[
            [pltpu.VMEM((2, TIMES, 2, 2, 32, vecs), F32) for _ in range(moms)],
            pltpu.VMEM((2, pairs, 2, cols, 2 * vecs), F32),
            pltpu.VMEM((moms * cols * pairs * 8, vecs), F32),
            pltpu.SemaphoreType.DMA((moms, pairs)),
            pltpu.SMEM(time_pairs.shape, jnp.int32),
            pltpu.SMEM(momenta.shape, jnp.int32),
            pltpu.VMEM(eig_rows.shape, F32),
            pltpu.VMEM(per_rows.shape, F32),
            pltpu.SemaphoreType.DMA((4,)),
            pltpu.VMEM((2, 4 * vecs, depth), BF16),
            pltpu.VMEM((depth, 2 * vecs), BF16),
            pltpu.VMEM((depth, 2 * vecs), BF16),
            pltpu.VMEM((2 * vecs, depth), F32),
            pltpu.VMEM((2 * moms, depth), F32),
            pltpu.VMEM((moms, 2, 2, 2, 32, vecs), F32),
            pltpu.VMEM((moms, 3, 2, 32, vecs), F32),
            pltpu.VMEM((moms, 2, 32, vecs), F32),
            pltpu.VMEM((moms, 2, 32, vecs), F32),
            pltpu.VMEM((pairs, 2, cols, 2 * vecs), F32),
            pltpu.VMEM((pairs, 2, cols, 2 * vecs), F32),
            pltpu.SemaphoreType.DMA((moms, 15)),
            pltpu.SemaphoreType.DMA((moms, 15)),
            pltpu.SemaphoreType.DMA((2, pairs, cols // 8)),
            pltpu.SemaphoreType.DMA((2, pairs, cols // 8)),
        ],
        compiler_params=pltpu.CompilerParams(
            collective_id=0, has_side_effects=True, vmem_limit_bytes=61 * 2**20
        ),
        name="correlators",
    )(momenta, eig_rows, per_rows, time_pairs)
    rows = pl.pallas_call(
        copy_kernel,
        out_shape=jax.ShapeDtypeStruct(rows.shape, F32),
        in_specs=[hbm],
        out_specs=hbm,
        scratch_shapes=[
            pltpu.VMEM(rows.shape, F32),
            pltpu.SemaphoreType.DMA((PARTS,)),
            pltpu.SemaphoreType.DMA((PARTS,)),
        ],
        compiler_params=pltpu.CompilerParams(vmem_limit_bytes=62 * 2**20),
        name="result",
    )(rows)
    return (
        rows.reshape(cols, pairs, moms, 4, 2, vecs)
        .transpose(0, 1, 2, 4, 3, 5)
        .reshape(cols, pairs, moms, 2, order)
    )


PRECISE = lax.Precision.HIGHEST
SPIN_MIX = ((1.0, 0.0, 1.0, 0.0), (0.0, 1.0, 0.0, 1.0), (1.0, 0.0, 1.0, 0.0), (0.0, 1.0, 0.0, 1.0))
CHIRAL = (1.0, 1.0, -1.0, -1.0)


def spin_tables():
    spin_mix = jnp.array(SPIN_MIX, jnp.float32)
    chiral = jnp.array(CHIRAL, jnp.float32)
    spin_dressed = chiral[:, None] * spin_mix * chiral[None, :]
    return (spin_mix, spin_dressed)


def phase_tables(momenta, site_ids):
    coords = jnp.stack([site_ids % LS, site_ids // LS % LS, site_ids // (LS * LS)])
    phase_turns = jnp.mod(jnp.sum(momenta[:, :, None] * coords[None, :, :], axis=1), LS)
    phase_angle = phase_turns.astype(jnp.float32) * (2.0 * math.pi / LS)
    return (jnp.cos(phase_angle), jnp.sin(phase_angle))


def elemental_terms(vectors, cosine_tab, sine_tab):
    local_times = vectors.shape[0]
    vec_count = vectors.shape[4]
    real_part = vectors[:, :, :, 0, :]
    imag_part = vectors[:, :, :, 1, :]
    left_rows = vectors.reshape(local_times, -1, vec_count)
    per_moment = []
    for mom_index in range(cosine_tab.shape[0]):
        cos_here = cosine_tab[mom_index][None, None, :, None]
        sin_here = sine_tab[mom_index][None, None, :, None]
        turned_re = cos_here * real_part - sin_here * imag_part
        turned_im = sin_here * real_part + cos_here * imag_part
        first_half = jnp.stack([turned_re, turned_im], axis=3).reshape(local_times, -1, vec_count)
        second_half = jnp.stack([turned_im, -turned_re], axis=3).reshape(local_times, -1, vec_count)
        right_cols = jnp.concatenate([first_half, second_half], axis=2)
        product = jnp.einsum("tki,tkj->tij", left_rows, right_cols, precision=PRECISE)
        per_moment.append(
            product.reshape(local_times, vec_count, 2, vec_count).transpose(0, 2, 1, 3)
        )
    return jnp.stack(per_moment, axis=1)


def shards(eigvecs, perambulator, time_pairs, momenta):
    colour_count = eigvecs.shape[1]
    site_count = eigvecs.shape[2]
    vec_count = eigvecs.shape[4]
    slab_count = lax.axis_size("slab")
    site_ids = lax.axis_index("slab") * site_count + jnp.arange(site_count, dtype=jnp.int32)
    cosine_tab, sine_tab = phase_tables(momenta, site_ids)
    partial_sums = elemental_terms(eigvecs, cosine_tab, sine_tab)
    summed = lax.psum(partial_sums, "slab")
    all_times = lax.all_gather(summed, "tm", axis=0, tiled=True)
    all_times = all_times * (1.0 / math.sqrt(2.0 * colour_count * site_count * slab_count))
    sink_elem = jnp.take(all_times, time_pairs[:, 1], axis=0)
    source_elem = jnp.take(all_times, time_pairs[:, 0], axis=0)
    sink_re = sink_elem[:, :, 0]
    sink_im = sink_elem[:, :, 1]
    spin_mix, spin_dressed = spin_tables()
    panel_cols = perambulator.shape[0]
    pair_count = perambulator.shape[1]
    spin_order = perambulator.shape[3]
    spin_count = spin_order // vec_count
    mom_count = momenta.shape[0]
    panel_start = lax.axis_index("slab") * panel_cols
    panel_spin = panel_start // vec_count
    panel_vec = panel_start % vec_count
    chiral_col = lax.dynamic_index_in_dim(spin_dressed, panel_spin, 1, keepdims=False)
    source_block = lax.dynamic_slice_in_dim(source_elem, panel_vec, panel_cols, 3)
    dress_re = jnp.einsum("s,kmbi->kmsib", chiral_col, source_block[:, :, 0]).reshape(
        pair_count, mom_count, spin_order, panel_cols
    )
    dress_im = -jnp.einsum("s,kmbi->kmsib", chiral_col, source_block[:, :, 1]).reshape(
        pair_count, mom_count, spin_order, panel_cols
    )
    peram_piece = lax.all_gather(perambulator, "slab", axis=0, tiled=True)
    piece_re = peram_piece[:, :, 0]
    piece_im = peram_piece[:, :, 1]
    fold_re = jnp.einsum("ckr,kmcb->bkmr", piece_re, dress_re, precision=PRECISE) - jnp.einsum(
        "ckr,kmcb->bkmr", piece_im, dress_im, precision=PRECISE
    )
    fold_im = jnp.einsum("ckr,kmcb->bkmr", piece_re, dress_im, precision=PRECISE) + jnp.einsum(
        "ckr,kmcb->bkmr", piece_im, dress_re, precision=PRECISE
    )
    fold_re, fold_im = (fold_re, fold_im)
    fold_re = fold_re.reshape(panel_cols, pair_count, mom_count, spin_count, vec_count)
    fold_im = fold_im.reshape(panel_cols, pair_count, mom_count, spin_count, vec_count)
    mixed_re = jnp.einsum("bkmsj,kmij->bkmsi", fold_re, sink_re, precision=PRECISE) - jnp.einsum(
        "bkmsj,kmij->bkmsi", fold_im, sink_im, precision=PRECISE
    )
    mixed_im = jnp.einsum("bkmsj,kmij->bkmsi", fold_re, sink_im, precision=PRECISE) + jnp.einsum(
        "bkmsj,kmij->bkmsi", fold_im, sink_re, precision=PRECISE
    )
    final_re = jnp.einsum("ts,bkmsi->bkmti", spin_mix, mixed_re, precision=PRECISE).reshape(
        panel_cols, pair_count, mom_count, spin_order
    )
    final_im = jnp.einsum("ts,bkmsi->bkmti", spin_mix, mixed_im, precision=PRECISE).reshape(
        panel_cols, pair_count, mom_count, spin_order
    )
    dressed = jnp.stack([final_re, final_im], axis=3)
    return dressed


def solution(mesh):
    known = mesh.shape["tm"] == TIMES and mesh.shape["slab"] == SLABS
    return jax.shard_map(
        kernel_shards if known else shards,
        mesh=mesh,
        in_specs=(
            P("tm", None, "slab", None, None),
            P("slab", "tm", None, None),
            P("tm", None),
            P(),
        ),
        out_specs=P("slab", "tm", None, None, None),
        check_vma=False,
    )
```

```python
import functools
import math

import jax
import jax.numpy as jnp
from jax import lax
from jax.experimental import pallas as pl
from jax.experimental.pallas import tpu as pltpu
from jax.sharding import PartitionSpec as P

LS = 48
SLABS = 8
TIMES = 4
PARTS = 4
BF16 = jnp.bfloat16
F32 = jnp.float32
NN = (((1,), (0,)), ((), ()))
NT = (((1,), (1,)), ((), ()))


def split(value):
    high = value.astype(BF16)
    return high, (value - high.astype(F32)).astype(BF16)


def dot3(left, right, dims):
    def one(x, y):
        return lax.dot_general(x, y, dims, preferred_element_type=F32)

    return one(left[0], right[0]) + (one(left[0], right[1]) + one(left[1], right[0]))


def floor_div(value, by):
    return jnp.floor((value + 0.5) * (1.0 / by))


def correlator_kernel(
    scale, sites, mom_hbm, eig_hbm, per_hbm, pairs_hbm, out_hbm,
    e_refs, d_ref, out_ref, out_sem, pairs_ref, mom_ref, eig_ref, per_ref, load_sem, left, rh, rl, flat, phase, part, r1, h2, r3, psend, precv,
    send_sem, recv_sem, psend_sem, precv_sem,
):
    slab = lax.axis_index("slab")
    time = lax.axis_index("tm")
    core = slab % 2
    sub = (slab // 2) % 2
    sibling = slab + 1 - 2 * core
    near = slab + 2 - 4 * sub
    cross = near + 1 - 2 * core
    far = (slab + 4) % SLABS
    tm_peers = (time + 1 - 2 * (time % 2), (time + 2) % TIMES, TIMES - 1 - time)
    slab_peers = (sibling, near, cross, far)

    loads = [
        pltpu.make_async_copy(src, dst, load_sem.at[n])
        for n, (src, dst) in enumerate(
            ((per_hbm, per_ref), (mom_hbm, mom_ref), (eig_hbm, eig_ref), (pairs_hbm, pairs_ref))
        )
    ]
    for load in loads:
        load.start()

    barrier = pltpu.get_barrier_semaphore()
    for peer in slab_peers:
        pl.semaphore_signal(barrier, inc=1, device_id={"slab": peer}, device_id_type=pl.DeviceIdType.MESH)
    for peer in tm_peers:
        pl.semaphore_signal(barrier, inc=1, device_id={"tm": peer}, device_id_type=pl.DeviceIdType.MESH)

    loads[0].wait()
    pairs = psend.shape[0]
    cols = psend.shape[2]
    for k in range(pairs):
        for p in range(2):
            spins = [
                per_ref[pl.ds(k * 8 + t * 2 + p, cols, stride=8 * pairs), :] for t in range(4)
            ]
            psend[k, p, :, 0:128] = spins[0] + spins[2]
            psend[k, p, :, 128:256] = spins[1] + spins[3]

    pl.semaphore_wait(barrier, len(slab_peers) + len(tm_peers))

    def remote(src, dst, ssem, rsem, axis, peer):
        return pltpu.make_async_remote_copy(
            src_ref=src, dst_ref=dst, send_sem=ssem, recv_sem=rsem,
            device_id={axis: peer}, device_id_type=pl.DeviceIdType.MESH,
        )

    p_far = [
        remote(psend.at[k], precv.at[k], psend_sem.at[0, k], precv_sem.at[0, k], "slab", far)
        for k in range(pairs)
    ]
    p_core = [
        remote(d_ref.at[core, k], d_ref.at[core, k], psend_sem.at[1, k], precv_sem.at[1, k], "slab", sibling)
        for k in range(pairs)
    ]

    def difference(k):
        p_far[k].wait_recv()
        d_ref[core, k] = psend[k] - precv[k]
        p_core[k].start()

    p_far[0].start()
    loads[1].wait()

    moms = mom_ref.shape[0]
    colours = eig_ref.shape[0] // (2 * sites)
    depth = colours * sites
    place = lax.broadcasted_iota(jnp.int32, (2 * moms, depth), 1).astype(F32)
    kind = lax.broadcasted_iota(jnp.int32, (2 * moms, depth), 0)
    site = place - sites * floor_div(place, sites) + (slab * sites).astype(F32)
    row = floor_div(site, LS)
    plane = floor_div(row, LS)
    coords = (site - LS * row, row - LS * plane, plane)
    turns = jnp.zeros((2 * moms, depth), F32)
    for m in range(moms):
        mine = mom_ref[m, 0].astype(F32) * coords[0]
        mine = mine + mom_ref[m, 1].astype(F32) * coords[1]
        mine = mine + mom_ref[m, 2].astype(F32) * coords[2]
        turns = jnp.where(kind % moms == m, mine, turns)
    turns = turns - LS * floor_div(turns, LS)
    turns = jnp.where(kind >= moms, turns - LS / 4, turns)
    phase[...] = jnp.cos(turns * (2.0 * math.pi / LS))

    loads[2].wait()
    vecs = eig_ref.shape[1]
    wide = 2 * vecs
    rows = []
    for c in range(colours):
        real = eig_ref[pl.ds(2 * sites * c, sites, stride=2), :]
        imag = eig_ref[pl.ds(2 * sites * c + 1, sites, stride=2), :]
        rows.append(jnp.concatenate([real, imag], axis=1))
    whole = jnp.concatenate(rows, axis=0)
    high, low = split(whole)
    rh[...] = high
    rl[...] = low
    flat[...] = whole.T

    def turn(m):
        cosine = phase[m:m + 1, :]
        sine = phase[moms + m:moms + m + 1, :]
        real = flat[:vecs, :]
        imag = flat[vecs:, :]
        slot = m % 2
        for n, value in enumerate(
            (cosine * real - sine * imag, sine * real + cosine * imag)
        ):
            high, low = split(value)
            left[slot, n * vecs:(n + 1) * vecs] = high
            left[slot, wide + n * vecs:wide + (n + 1) * vecs] = low

    def compute(m):
        slot = m % 2
        coarse = lax.dot_general(left[slot], rh[...], NN, preferred_element_type=F32)
        fine = lax.dot_general(left[slot, :wide], rl[...], NN, preferred_element_type=F32)
        if m + 1 < moms:
            turn(m + 1)
        got = coarse[:wide] + (coarse[wide:] + fine)
        both = (
            (got[:vecs, :vecs] + got[vecs:, vecs:]).T,
            (got[vecs:, :vecs] - got[:vecs, vecs:]).T,
        )
        for half in range(2):
            for u in range(2):
                for p in range(2):
                    start = half * 64 + u * 32
                    part[m, half, u, p] = both[p][start:start + 32]

    steps = {}

    def step1(m):
        for n, (half, u, peer) in enumerate(
            ((1 - core, sub, sibling), (core, 1 - sub, near), (1 - core, 1 - sub, cross))
        ):
            steps[m, 1, n] = remote(
                part.at[m, half, u], r1.at[m, n], send_sem.at[m, n], recv_sem.at[m, n], "slab", peer
            )
            steps[m, 1, n].start()

    def step2(m):
        for n in range(3):
            steps[m, 1, n].wait_recv()
        h2[m] = (part[m, core, sub] + r1[m, 0]) + (r1[m, 1] + r1[m, 2])
        steps[m, 2] = remote(h2.at[m], r3.at[m], send_sem.at[m, 3], recv_sem.at[m, 3], "slab", far)
        steps[m, 2].start()

    def step3(m):
        steps[m, 2].wait_recv()
        e_refs[m][core, time, sub] = (h2[m] + r3[m]) * scale
        done = e_refs[m].at[core, time, sub]
        steps[m, 3] = remote(done, done, send_sem.at[m, 4], recv_sem.at[m, 4], "slab", near)
        steps[m, 3].start()

    def step4(m):
        steps[m, 3].wait_recv()
        done = e_refs[m].at[core, time]
        for n, peer in enumerate(tm_peers):
            steps[m, 4, n] = remote(
                done, done, send_sem.at[m, 5 + n], recv_sem.at[m, 5 + n], "tm", peer
            )
            steps[m, 4, n].start()

    def step5(m):
        for n in range(len(tm_peers)):
            steps[m, 4, n].wait_recv()
        done = e_refs[m].at[core]
        steps[m, 5] = remote(done, done, send_sem.at[m, 8], recv_sem.at[m, 8], "slab", sibling)
        steps[m, 5].start()

    def step6(m):
        steps[m, 5].wait_recv()

    rows_each = cols * 8

    def dress(m, k):
        e_ref = e_refs[m]
        t1 = pairs_ref[k, 0]
        t2 = pairs_ref[k, 1]

        def block(half, t, p):
            return e_ref[half, t, :, p].reshape(64, 128)

        source = split(jnp.concatenate([block(core, t1, 0), block(core, t1, 1)], axis=1))
        re_high, re_low = split(d_ref[:, k, 0].reshape(2 * cols, 256))
        im_high, im_low = split(d_ref[:, k, 1].reshape(2 * cols, 256))

        def wide_of(re, im):
            return jnp.concatenate(
                [jnp.concatenate([re, im], axis=1), jnp.concatenate([im, -re], axis=1)], axis=0
            )

        fold = dot3(source, (wide_of(re_high, im_high), wide_of(re_low, im_low)), NN)
        spun = jnp.concatenate(
            [
                jnp.concatenate([fold[:, 0:128], fold[:, 256:384]], axis=1),
                jnp.concatenate([fold[:, 128:256], fold[:, 384:512]], axis=1),
            ],
            axis=0,
        )
        sink = [
            split(jnp.concatenate([block(0, t2, p), block(1, t2, p)], axis=0)) for p in range(2)
        ]

        def tall_of(re, im):
            return jnp.concatenate(
                [jnp.concatenate([re, -im], axis=1), jnp.concatenate([im, re], axis=1)], axis=0
            )

        right = tuple(tall_of(sink[0][n], sink[1][n]) for n in range(2))
        got = dot3(split(spun), right, NT)
        for t in range(4):
            for p in range(2):
                start = (m * pairs + k) * rows_each + t * 2 + p
                out_ref[pl.ds(start, cols, stride=8), :] = got[
                    64 * (t % 2):64 * (t % 2 + 1), 128 * p:128 * (p + 1)
                ]
        stores[m, k] = pltpu.make_async_copy(
            out_ref.at[pl.ds((m * pairs + k) * rows_each, rows_each)].reshape(cols, 8, 128),
            out_hbm.at[:, k, m],
            out_sem.at[m, k],
        )
        stores[m, k].start()

    stores = {}
    stages = (step1, step2, step3, step4, step5, step6)
    loads[3].wait()
    turn(0)
    ticks = moms + len(stages) - 1
    for tick in range(ticks - 1):
        if tick < moms:
            compute(tick)
        if tick == moms - 1:
            for k in range(1, pairs):
                p_far[k].start()
        arrived = None
        for m in range(moms):
            if 0 <= tick - m < len(stages):
                stages[tick - m](m)
                if stages[tick - m] is step6:
                    arrived = m
        if tick == moms:
            difference(0)
        if tick == ticks - 3:
            for k in range(1, pairs):
                difference(k)
        if arrived is not None:
            if arrived == 0:
                p_core[0].wait_recv()
            dress(arrived, 0)
    for k in range(1, pairs):
        p_core[k].wait_recv()
        for m in range(moms - 1):
            dress(m, k)
    step6(moms - 1)
    for k in range(pairs):
        dress(moms - 1, k)

    for copy in p_far + p_core:
        copy.wait_send()
    for copy in steps.values():
        copy.wait_send()
    for store in stores.values():
        store.wait()


def copy_kernel(src, dst, held, in_sem, out_sem):
    share = src.shape[0] // PARTS
    loads, stores = [], []
    for n in range(PARTS):
        part = pl.ds(n * share, share)
        loads.append(pltpu.make_async_copy(src.at[part], held.at[part], in_sem.at[n]))
        stores.append(pltpu.make_async_copy(held.at[part], dst.at[part], out_sem.at[n]))
    for load in loads:
        load.start()
    for load, store in zip(loads, stores):
        load.wait()
        store.start()
    for store in stores:
        store.wait()


def kernel_shards(eigvecs, perambulator, time_pairs, momenta):
    _, colours, sites, _, vecs = eigvecs.shape
    cols, pairs, _, order = perambulator.shape
    moms = momenta.shape[0]
    scale = 1.0 / math.sqrt(2.0 * colours * sites * SLABS)
    eig_rows = eigvecs.reshape(colours * sites * 2, vecs)
    per_rows = (
        perambulator.reshape(cols, pairs, 2, 4, vecs)
        .transpose(0, 1, 3, 2, 4)
        .reshape(cols * pairs * 8, vecs)
    )
    depth = colours * sites
    hbm = pl.BlockSpec(memory_space=pltpu.HBM)
    rows = pl.pallas_call(
        functools.partial(correlator_kernel, scale, sites),
        out_shape=jax.ShapeDtypeStruct((cols, pairs, moms, 8, vecs), F32),
        in_specs=[hbm, hbm, hbm, hbm],
        out_specs=hbm,
        scratch_shapes=[
            [pltpu.VMEM((2, TIMES, 2, 2, 32, vecs), F32) for _ in range(moms)],
            pltpu.VMEM((2, pairs, 2, cols, 2 * vecs), F32),
            pltpu.VMEM((moms * cols * pairs * 8, vecs), F32),
            pltpu.SemaphoreType.DMA((moms, pairs)),
            pltpu.SMEM(time_pairs.shape, jnp.int32),
            pltpu.SMEM(momenta.shape, jnp.int32),
            pltpu.VMEM(eig_rows.shape, F32),
            pltpu.VMEM(per_rows.shape, F32),
            pltpu.SemaphoreType.DMA((4,)),
            pltpu.VMEM((2, 4 * vecs, depth), BF16),
            pltpu.VMEM((depth, 2 * vecs), BF16),
            pltpu.VMEM((depth, 2 * vecs), BF16),
            pltpu.VMEM((2 * vecs, depth), F32),
            pltpu.VMEM((2 * moms, depth), F32),
            pltpu.VMEM((moms, 2, 2, 2, 32, vecs), F32),
            pltpu.VMEM((moms, 3, 2, 32, vecs), F32),
            pltpu.VMEM((moms, 2, 32, vecs), F32),
            pltpu.VMEM((moms, 2, 32, vecs), F32),
            pltpu.VMEM((pairs, 2, cols, 2 * vecs), F32),
            pltpu.VMEM((pairs, 2, cols, 2 * vecs), F32),
            pltpu.SemaphoreType.DMA((moms, 9)),
            pltpu.SemaphoreType.DMA((moms, 9)),
            pltpu.SemaphoreType.DMA((2, pairs)),
            pltpu.SemaphoreType.DMA((2, pairs)),
        ],
        compiler_params=pltpu.CompilerParams(
            collective_id=0, has_side_effects=True, vmem_limit_bytes=61 * 2**20
        ),
        name="correlators",
    )(momenta, eig_rows, per_rows, time_pairs)
    rows = pl.pallas_call(
        copy_kernel,
        out_shape=jax.ShapeDtypeStruct(rows.shape, F32),
        in_specs=[hbm],
        out_specs=hbm,
        scratch_shapes=[
            pltpu.VMEM(rows.shape, F32),
            pltpu.SemaphoreType.DMA((PARTS,)),
            pltpu.SemaphoreType.DMA((PARTS,)),
        ],
        compiler_params=pltpu.CompilerParams(vmem_limit_bytes=62 * 2**20),
        name="result",
    )(rows)
    return (
        rows.reshape(cols, pairs, moms, 4, 2, vecs)
        .transpose(0, 1, 2, 4, 3, 5)
        .reshape(cols, pairs, moms, 2, order)
    )


PRECISE = lax.Precision.HIGHEST
SPIN_MIX = ((1.0, 0.0, 1.0, 0.0), (0.0, 1.0, 0.0, 1.0), (1.0, 0.0, 1.0, 0.0), (0.0, 1.0, 0.0, 1.0))
CHIRAL = (1.0, 1.0, -1.0, -1.0)


def spin_tables():
    spin_mix = jnp.array(SPIN_MIX, jnp.float32)
    chiral = jnp.array(CHIRAL, jnp.float32)
    spin_dressed = chiral[:, None] * spin_mix * chiral[None, :]
    return (spin_mix, spin_dressed)


def phase_tables(momenta, site_ids):
    coords = jnp.stack([site_ids % LS, site_ids // LS % LS, site_ids // (LS * LS)])
    phase_turns = jnp.mod(jnp.sum(momenta[:, :, None] * coords[None, :, :], axis=1), LS)
    phase_angle = phase_turns.astype(jnp.float32) * (2.0 * math.pi / LS)
    return (jnp.cos(phase_angle), jnp.sin(phase_angle))


def elemental_terms(vectors, cosine_tab, sine_tab):
    local_times = vectors.shape[0]
    vec_count = vectors.shape[4]
    real_part = vectors[:, :, :, 0, :]
    imag_part = vectors[:, :, :, 1, :]
    left_rows = vectors.reshape(local_times, -1, vec_count)
    per_moment = []
    for mom_index in range(cosine_tab.shape[0]):
        cos_here = cosine_tab[mom_index][None, None, :, None]
        sin_here = sine_tab[mom_index][None, None, :, None]
        turned_re = cos_here * real_part - sin_here * imag_part
        turned_im = sin_here * real_part + cos_here * imag_part
        first_half = jnp.stack([turned_re, turned_im], axis=3).reshape(local_times, -1, vec_count)
        second_half = jnp.stack([turned_im, -turned_re], axis=3).reshape(local_times, -1, vec_count)
        right_cols = jnp.concatenate([first_half, second_half], axis=2)
        product = jnp.einsum("tki,tkj->tij", left_rows, right_cols, precision=PRECISE)
        per_moment.append(
            product.reshape(local_times, vec_count, 2, vec_count).transpose(0, 2, 1, 3)
        )
    return jnp.stack(per_moment, axis=1)


def shards(eigvecs, perambulator, time_pairs, momenta):
    colour_count = eigvecs.shape[1]
    site_count = eigvecs.shape[2]
    vec_count = eigvecs.shape[4]
    slab_count = lax.axis_size("slab")
    site_ids = lax.axis_index("slab") * site_count + jnp.arange(site_count, dtype=jnp.int32)
    cosine_tab, sine_tab = phase_tables(momenta, site_ids)
    partial_sums = elemental_terms(eigvecs, cosine_tab, sine_tab)
    summed = lax.psum(partial_sums, "slab")
    all_times = lax.all_gather(summed, "tm", axis=0, tiled=True)
    all_times = all_times * (1.0 / math.sqrt(2.0 * colour_count * site_count * slab_count))
    sink_elem = jnp.take(all_times, time_pairs[:, 1], axis=0)
    source_elem = jnp.take(all_times, time_pairs[:, 0], axis=0)
    sink_re = sink_elem[:, :, 0]
    sink_im = sink_elem[:, :, 1]
    spin_mix, spin_dressed = spin_tables()
    panel_cols = perambulator.shape[0]
    pair_count = perambulator.shape[1]
    spin_order = perambulator.shape[3]
    spin_count = spin_order // vec_count
    mom_count = momenta.shape[0]
    panel_start = lax.axis_index("slab") * panel_cols
    panel_spin = panel_start // vec_count
    panel_vec = panel_start % vec_count
    chiral_col = lax.dynamic_index_in_dim(spin_dressed, panel_spin, 1, keepdims=False)
    source_block = lax.dynamic_slice_in_dim(source_elem, panel_vec, panel_cols, 3)
    dress_re = jnp.einsum("s,kmbi->kmsib", chiral_col, source_block[:, :, 0]).reshape(
        pair_count, mom_count, spin_order, panel_cols
    )
    dress_im = -jnp.einsum("s,kmbi->kmsib", chiral_col, source_block[:, :, 1]).reshape(
        pair_count, mom_count, spin_order, panel_cols
    )
    peram_piece = lax.all_gather(perambulator, "slab", axis=0, tiled=True)
    piece_re = peram_piece[:, :, 0]
    piece_im = peram_piece[:, :, 1]
    fold_re = jnp.einsum("ckr,kmcb->bkmr", piece_re, dress_re, precision=PRECISE) - jnp.einsum(
        "ckr,kmcb->bkmr", piece_im, dress_im, precision=PRECISE
    )
    fold_im = jnp.einsum("ckr,kmcb->bkmr", piece_re, dress_im, precision=PRECISE) + jnp.einsum(
        "ckr,kmcb->bkmr", piece_im, dress_re, precision=PRECISE
    )
    fold_re, fold_im = (fold_re, fold_im)
    fold_re = fold_re.reshape(panel_cols, pair_count, mom_count, spin_count, vec_count)
    fold_im = fold_im.reshape(panel_cols, pair_count, mom_count, spin_count, vec_count)
    mixed_re = jnp.einsum("bkmsj,kmij->bkmsi", fold_re, sink_re, precision=PRECISE) - jnp.einsum(
        "bkmsj,kmij->bkmsi", fold_im, sink_im, precision=PRECISE
    )
    mixed_im = jnp.einsum("bkmsj,kmij->bkmsi", fold_re, sink_im, precision=PRECISE) + jnp.einsum(
        "bkmsj,kmij->bkmsi", fold_im, sink_re, precision=PRECISE
    )
    final_re = jnp.einsum("ts,bkmsi->bkmti", spin_mix, mixed_re, precision=PRECISE).reshape(
        panel_cols, pair_count, mom_count, spin_order
    )
    final_im = jnp.einsum("ts,bkmsi->bkmti", spin_mix, mixed_im, precision=PRECISE).reshape(
        panel_cols, pair_count, mom_count, spin_order
    )
    dressed = jnp.stack([final_re, final_im], axis=3)
    return dressed


def solution(mesh):
    known = mesh.shape["tm"] == TIMES and mesh.shape["slab"] == SLABS
    return jax.shard_map(
        kernel_shards if known else shards,
        mesh=mesh,
        in_specs=(
            P("tm", None, "slab", None, None),
            P("slab", "tm", None, None),
            P("tm", None),
            P(),
        ),
        out_specs=P("slab", "tm", None, None, None),
        check_vma=False,
    )
```
